32 devices in a mesh: dom: 2 (over x), leaf: 2 (over core), row: 8 (over z, y).
Axes of the slice: x: 2, y: 2, z: 4, core: 2. Of those that a mesh axis runs over, the one named last changes fastest.
Arguments:
- features: bfloat16 [128, 65536], P(None, ('dom', 'row')), parts along dimension 1, may hold values from -6 to 6
- targets: bfloat16 [32, 65536], P(None, ('dom', 'row')), parts along dimension 1, may hold values from -6 to 6
- bootstrap: int32 [2, 65536], P('leaf', ('dom', 'row')), parts along dimension 1, may hold values from 0 to 3
- node_ids: int32 [2, 65536], P('leaf', ('dom', 'row')), parts along dimension 1, may hold values from 0 to 35, as said below
- node_flags: int32 [2, 72], P('leaf', 'dom'), parts along dimension 1, may hold values from 0 to 1, as said below
- node_place: int32 [2, 72], P('leaf', 'dom'), parts along dimension 1, may hold values from 0 to 31, as said below
Outputs:
- large_gain: float32 [2, 8, 128], P('leaf', 'dom', 'row'), parts along dimension 1
- small_gain: float32 [2, 32, 256], P('leaf', 'row', 'dom'), parts along dimension 2
The draws below stay inside these ranges and needn't reach their ends.
There are 2 independent parts, one for each index of `dom`. The reference program is written for one: setup_inputs(seed, part) draws one part's arguments, and reference() takes and returns one part's arrays. A program takes and returns all parts, laid end to end along the dimension named above; each array names one. Nothing has to cross between parts.
Inputs may be any that keep to these rules, and one draw needn't show every extreme that they name: `node_flags`: every node of a tree is large or small, the 4 large ones flagged 1. `node_place`: the large nodes of a tree take the ranks 0 to 3 once each; the small nodes take the places 0 to 31 once each, place s belonging to builder s // 4 of the row axis. `node_ids`: among one device's rows of a tree, at most 256 belong to small nodes of any one builder; in every tree one builder has exactly 256 such rows on every device.
All inputs are finite; a program needn't handle non-finite values.
Results may differ from the reference program's by a relative error of at most 0.0012.
Values may be sent and summed in bfloat16 or wider, within the bound.
A program may use at most 192 MiB of HBM per device.

```python
import jax
import jax.numpy as jnp
from jax import lax

F = 128
B = 64
K = 32
NL = 4
SB = 4
ROWS_DEV = 4096
ROWS = 32768
CAP = 256
NS = 32
NODES = 36
TREES = 2
N_LEAF = 2
N_ROW = 8


def draw_layout(key):
    subkeys = jax.random.split(key, 8)
    scores = jax.random.randint(subkeys[0], (N_LEAF, NODES), 0, 2 ** 20, dtype=jnp.int32) * NODES
    scores = scores + jnp.arange(NODES, dtype=jnp.int32)[None, :]
    node_order = jnp.argsort(scores, axis=1, stable=True).astype(jnp.int32)
    node_ranks = jnp.arange(NODES, dtype=jnp.int32)
    place_value = jnp.where(node_ranks < NL, node_ranks, node_ranks - NL)
    flag_value = (node_ranks < NL).astype(jnp.int32)
    tree_rows = jnp.arange(N_LEAF, dtype=jnp.int32)[:, None]
    flag_table = jnp.zeros((N_LEAF, NODES), jnp.int32).at[tree_rows, node_order].set(jnp.broadcast_to(flag_value, (N_LEAF, NODES)))
    place_table = jnp.zeros((N_LEAF, NODES), jnp.int32).at[tree_rows, node_order].set(jnp.broadcast_to(place_value, (N_LEAF, NODES)))
    is_heavy = jax.random.randint(subkeys[1], (N_LEAF, N_ROW), 0, 8, dtype=jnp.int32) == 0
    full_builder = jax.random.randint(subkeys[2], (N_LEAF, 1), 0, N_ROW, dtype=jnp.int32)
    high_counts = jax.random.randint(subkeys[3], (N_LEAF, N_ROW, N_ROW), CAP // 2, CAP + 1, dtype=jnp.int32)
    low_counts = jax.random.randint(subkeys[4], (N_LEAF, N_ROW, N_ROW), CAP // 4, CAP // 2 + 1, dtype=jnp.int32)
    per_builder = jnp.where(is_heavy[:, None, :], high_counts, low_counts)
    builder_ids = jnp.arange(N_ROW, dtype=jnp.int32)
    per_builder = jnp.where(builder_ids[None, None, :] == full_builder[:, :, None], CAP, per_builder)
    builder_ends = jnp.cumsum(per_builder, axis=-1)
    row_spots = jnp.arange(ROWS_DEV, dtype=jnp.int32)
    builder = jnp.sum((builder_ends[:, :, None, :] <= row_spots[None, None, :, None]).astype(jnp.int32), axis=-1)
    node_slot = jax.random.randint(subkeys[5], (N_LEAF, N_ROW, ROWS_DEV), 0, SB, dtype=jnp.int32)
    large_pick = jax.random.randint(subkeys[6], (N_LEAF, N_ROW, ROWS_DEV), 0, NL, dtype=jnp.int32)
    pick_index = jnp.where(builder < N_ROW, NL + builder * SB + node_slot, large_pick)
    node_table = jnp.take_along_axis(node_order, pick_index.reshape(N_LEAF, -1), axis=1)
    node_table = node_table.reshape(N_LEAF, N_ROW, ROWS_DEV)
    shuffle = jax.random.randint(subkeys[7], (N_LEAF, N_ROW, ROWS_DEV), 0, 2 ** 31 // ROWS_DEV - 1, dtype=jnp.int32) * ROWS_DEV + row_spots[None, None, :]
    row_order = jnp.argsort(shuffle, axis=-1, stable=True)
    node_table = jnp.take_along_axis(node_table, row_order, axis=-1)
    return (flag_table, place_table, node_table.reshape(N_LEAF, N_ROW * ROWS_DEV).astype(jnp.int32))


def draw_node_ids(key, part):
    return draw_layout(key)[2]


def draw_node_flags(key, part):
    return draw_layout(key)[0]


def draw_node_place(key, part):
    return draw_layout(key)[1]


def plant(entries, key, low, largest):
    longest = entries.shape.index(max(entries.shape))
    spots = []
    for shift in (0, 1):
        where = [jax.random.randint(jax.random.fold_in(key, axis), (), 0, length) for axis, length in enumerate(entries.shape)]
        where[longest] = (where[longest] + shift) % entries.shape[longest]
        spots.append(tuple(where))
    return entries.at[spots[0]].set(low).at[spots[1]].set(largest)


def steps_of(stream_key, dims, shards, smallest, high):
    def one(axis_at, blocks):
        draws = jax.random.uniform(jax.random.fold_in(jax.random.fold_in(stream_key, 6), axis_at), (blocks,), jnp.float32, smallest / len(shards), high / len(shards))
        return jnp.repeat(jnp.exp(draws), dims[axis_at] // blocks).reshape((-1,) + (1,) * (len(dims) - axis_at - 1))

    loudness = one(*shards[0])
    for cut in shards[1:]:
        loudness = loudness * one(*cut)
    return loudness


def centred(stream_key, extent, scale, limit, cuts=(), kind=jnp.bfloat16):
    drawn = jax.random.normal(stream_key, extent, jnp.float32) * scale
    if len(cuts) > 0:
        drawn = steps_of(stream_key, extent, cuts, -0.22, 0.18) * drawn
    return jnp.clip(drawn, min=-limit, max=limit).astype(kind)


def setup_inputs(seed: int = 0, part: int = 0) -> dict:
    arg_keys = jax.random.split(jax.random.key(seed), 7)
    part_splits = jax.random.split(jax.random.fold_in(arg_keys[6], part), 7)
    return {
        "features": centred(part_splits[0], (F, ROWS), 1.0, 6.0, ((1, 8),)),
        "targets": centred(part_splits[1], (K, ROWS), 1.0, 6.0, ((1, 8),)),
        "bootstrap": plant(jax.random.randint(part_splits[2], (TREES, ROWS), 0, 4), jax.random.fold_in(part_splits[2], 1), 0, 3).astype(jnp.int32),
        "node_ids": draw_node_ids(jax.random.fold_in(jax.random.fold_in(arg_keys[6], part), 71), part),
        "node_flags": draw_node_flags(jax.random.fold_in(jax.random.fold_in(arg_keys[6], part), 71), part),
        "node_place": draw_node_place(jax.random.fold_in(jax.random.fold_in(arg_keys[6], part), 71), part),
    }


def bin_codes(values, levels):
    scaled = jnp.floor(values.astype(jnp.float32) * (levels / 4.0)) + levels // 2
    return jnp.clip(scaled, 0, levels - 1).astype(jnp.int32)


def node_gain(bin_sums, bin_counts):
    left_sum = jnp.cumsum(bin_sums, axis=0)[:-1]
    whole_sum = jnp.sum(bin_sums, axis=0)
    right_sum = whole_sum[None] - left_sum
    left_cnt = jnp.cumsum(bin_counts, axis=0)[:-1]
    whole_cnt = jnp.sum(bin_counts, axis=0)
    right_cnt = whole_cnt[None] - left_cnt
    scores = jnp.sum(left_sum * left_sum, axis=-1) / jnp.maximum(left_cnt, 1.0)
    scores = scores + jnp.sum(right_sum * right_sum, axis=-1) / jnp.maximum(right_cnt, 1.0)
    scores = scores - (jnp.sum(whole_sum * whole_sum, axis=-1) / jnp.maximum(whole_cnt, 1.0))[None]
    return jnp.max(scores, axis=0) / K


def reference(features, targets, bootstrap, node_ids, node_flags, node_place):
    row_codes = bin_codes(features, B)
    large_list = []
    small_list = []
    dump_segment = B * (NL + NS)
    for tree_idx in range(N_LEAF):
        weight = bootstrap[tree_idx].astype(jnp.float32)
        rounded = (targets.astype(jnp.float32) * weight[None, :]).astype(jnp.bfloat16)
        rounded = lax.optimization_barrier(rounded)
        weighted = rounded.astype(jnp.float32).T
        row_node = node_ids[tree_idx]
        is_large = node_flags[tree_idx][row_node] == 1
        position = node_place[tree_idx][row_node]

        def per_feature(feature_codes):
            segment = jnp.where(is_large & (position < NL), feature_codes * NL + position,
                                jnp.where(jnp.logical_not(is_large) & (position < NS),
                                          B * NL + feature_codes * NS + position, dump_segment))
            segment = segment.astype(jnp.int32)
            bin_sums = jax.ops.segment_sum(weighted, segment, num_segments=dump_segment + 1)
            bin_counts = jax.ops.segment_sum(weight, segment, num_segments=dump_segment + 1)
            large_part = node_gain(bin_sums[:B * NL].reshape(B, NL, K), bin_counts[:B * NL].reshape(B, NL))
            small_part = node_gain(bin_sums[B * NL:dump_segment].reshape(B, NS, K),
                                   bin_counts[B * NL:dump_segment].reshape(B, NS))
            return large_part, small_part

        large_part, small_part = lax.map(per_feature, row_codes)
        large_list.append(large_part.T)
        small_list.append(small_part.T)
    small_order = [small_list[(group_idx - 1) % N_LEAF] for group_idx in range(N_LEAF)]
    return jnp.stack(large_list), jnp.stack(small_order)
```

```python
import functools

import jax
import jax.numpy as jnp
from jax import lax
from jax.experimental import pallas as pl
from jax.experimental.pallas import tpu as pltpu
from jax.sharding import PartitionSpec as P

B = 64
NL = 4
SB = 4
FB = 16
TAIL = 16
NT = (((1,), (1,)), ((), ()))
VMEM = 50 * 1024 * 1024


def prep_kernel(row_devices, targets_ref, boot_ref, ids_ref, table_ref, pack_ref, rank_ref):
    width_k, rows = targets_ref.shape
    weight = boot_ref[...].astype(jnp.float32)
    weighted = (targets_ref[...].astype(jnp.float32) * weight).astype(jnp.bfloat16)
    nodes = table_ref.shape[1]
    node_hot = lax.broadcasted_iota(jnp.int32, (nodes, rows), 0) == ids_ref[...]
    node_hot = jnp.where(node_hot, 1.0, 0.0).astype(jnp.bfloat16)
    found = jnp.dot(table_ref[...], node_hot, preferred_element_type=jnp.float32)
    is_large = found[0:1] > 0.5
    place = found[1:2].astype(jnp.int32)
    large_label = jnp.where(is_large, place, NL).astype(jnp.float32)
    slot_label = (place % SB).astype(jnp.float32)
    dest = jnp.where(is_large, row_devices, place // SB)
    tail_row = lax.broadcasted_iota(jnp.int32, (TAIL, rows), 0)
    tail = jnp.where(tail_row == 0, weight, 0.0)
    tail = jnp.where(tail_row == 1, large_label, tail)
    tail = jnp.where(tail_row == 2, slot_label, tail)
    pack_ref[0:width_k, :] = weighted
    pack_ref[width_k : width_k + TAIL, :] = tail.astype(jnp.bfloat16)
    dest_rows = rank_ref.shape[0]
    step = 512
    earlier = lax.broadcasted_iota(jnp.int32, (step, step), 0) < lax.broadcasted_iota(
        jnp.int32, (step, step), 1
    )
    earlier = jnp.where(earlier, 1.0, 0.0).astype(jnp.bfloat16)
    carry = jnp.zeros((dest_rows, 1), jnp.float32)
    for at in range(0, rows, step):
        hot = lax.broadcasted_iota(jnp.int32, (dest_rows, step), 0) == dest[:, at : at + step]
        hot_f = jnp.where(hot, 1.0, 0.0)
        before = jnp.dot(hot_f.astype(jnp.bfloat16), earlier, preferred_element_type=jnp.float32)
        ranks = jnp.where(hot, before + carry, -1.0)
        rank_ref[:, 0, at : at + step] = ranks
        carry = carry + jnp.sum(hot_f, axis=1, keepdims=True)


def compact_kernel(pack_ref, features_ref, rank_ref, out_ref):
    rows = features_ref.shape[1]
    capacity = out_ref.shape[2]
    spots = lax.broadcasted_iota(jnp.int32, (capacity, 128), 0).astype(jnp.float32)
    spots = spots.astype(jnp.bfloat16)[:, 0:1]
    ranks = rank_ref[0].astype(jnp.bfloat16)
    hot = jnp.where(spots == ranks, 1.0, 0.0).astype(jnp.bfloat16)
    payload = jnp.concatenate([pack_ref[...], features_ref[...]], axis=0)
    moved = lax.dot_general(payload, hot, NT, preferred_element_type=jnp.float32)
    out_ref[0] = moved.astype(jnp.bfloat16)


def gain_kernel(width_k, label_row, pack_ref, features_ref, out_ref, acc_ref):
    at = pl.program_id(1)
    sources, _, rows = features_ref.shape
    step = min(rows, 512)

    @pl.when(at == 0)
    def _():
        acc_ref[...] = jnp.zeros_like(acc_ref)

    total = acc_ref[...]
    for source in range(sources):
        for start in range(0, rows, step):
            cut = pl.ds(start, step)
            weighted = pack_ref[source, 0:width_k, cut]
            tail = pack_ref[source, width_k : width_k + TAIL, cut]
            weight = tail[0:1]
            label = tail[label_row : label_row + 1]
            parts = [
                weighted * jnp.where(label == n, 1.0, 0.0).astype(jnp.bfloat16) for n in range(NL)
            ]
            node_row = lax.broadcasted_iota(jnp.int32, (TAIL, step), 0).astype(jnp.float32)
            parts.append(
                jnp.where(node_row == label.astype(jnp.float32), weight.astype(jnp.float32), 0.0)
                .astype(jnp.bfloat16)
            )
            columns = jnp.concatenate(parts, axis=0)
            values = features_ref[source, :, cut]
            one = jnp.ones_like(values)
            zero = jnp.zeros_like(values)
            masks = [
                jnp.where(values < jnp.bfloat16((u - B // 2 + 1) / 16.0), one, zero)
                for u in range(B - 1)
            ]
            masks.append(one)
            below = jnp.concatenate(masks, axis=0)
            total = total + lax.dot_general(columns, below, NT, preferred_element_type=jnp.float32)
    acc_ref[...] = total

    @pl.when(at == pl.num_programs(1) - 1)
    def _():
        wide = 128
        sums = NL * width_k
        pick = lax.broadcasted_iota(jnp.int32, (wide, wide), 0) == (
            wide - FB + lax.broadcasted_iota(jnp.int32, (wide, wide), 1) % FB
        )
        whole = jnp.dot(
            acc_ref[:, FB * B - wide : FB * B],
            jnp.where(pick, 1.0, 0.0),
            precision=lax.Precision.HIGHEST,
            preferred_element_type=jnp.float32,
        )
        whole_sum = whole[0:sums]
        whole_cnt = whole[sums : sums + 8]
        best = None
        for start in range(0, FB * B, wide):
            left_sum = acc_ref[0:sums, start : start + wide]
            left_cnt = acc_ref[sums : sums + 8, start : start + wide]
            right_sum = whole_sum - left_sum
            right_cnt = whole_cnt - left_cnt

            def term(vec, cnt):
                rows = []
                for n in range(NL):
                    part = vec[n * width_k : (n + 1) * width_k]
                    rows.append(jnp.sum(part * part, axis=0, keepdims=True))
                return jnp.concatenate(rows, axis=0) / jnp.maximum(cnt[0:NL], 1.0)

            score = term(left_sum, left_cnt) + term(right_sum, right_cnt)
            score = score - term(whole_sum, whole_cnt)
            if start == FB * B - wide:
                lane = lax.broadcasted_iota(jnp.int32, (NL, wide), 1)
                score = jnp.where(lane < wide - FB, score, -jnp.inf)
            best = score if best is None else jnp.maximum(best, score)
        out_ref[0] = best / width_k


def node_gains(pack, features, feat_row, feat_count, label_row, width_k, per_step):
    sources, pack_rows, rows = pack.shape[0], width_k + TAIL, pack.shape[2]
    blocks = feat_count // FB
    best = pl.pallas_call(
        functools.partial(gain_kernel, width_k, label_row),
        grid=(blocks, sources // per_step),
        in_specs=[
            pl.BlockSpec((per_step, pack_rows, rows), lambda j, i: (i, 0, 0)),
            pl.BlockSpec((per_step, FB, rows), lambda j, i: (i, feat_row // FB + j, 0)),
        ],
        out_specs=pl.BlockSpec((1, NL, 128), lambda j, i: (j, 0, 0)),
        out_shape=jax.ShapeDtypeStruct((blocks, NL, 128), jnp.float32),
        scratch_shapes=[pltpu.VMEM((NL * width_k + TAIL, FB * B), jnp.float32)],
        compiler_params=pltpu.CompilerParams(vmem_limit_bytes=VMEM),
        cost_estimate=pl.CostEstimate(
            flops=2 * feat_count * B * 144 * sources * rows,
            bytes_accessed=2 * sources * rows * (feat_count + 48),
            transcendentals=0,
        ),
    )(pack, features)
    best = jnp.max(best.reshape(blocks, NL, 128 // FB, FB), axis=2)
    return best.transpose(1, 0, 2).reshape(NL, feat_count)


def local(features, targets, bootstrap, node_ids, node_flags, node_place):
    feat_count, row_count = features.shape
    width_k = targets.shape[0]
    row_devices = lax.axis_size("row")
    leaf_devices = lax.axis_size("leaf")
    capacity = row_count // (2 * row_devices)
    own = feat_count // row_devices
    pack_rows = width_k + TAIL

    owned = lax.all_to_all(
        features.reshape(row_devices, own, row_count), "row", split_axis=0, concat_axis=0
    )
    owned = owned.reshape(row_devices, own, row_count)
    own_pad = -own % FB
    if own_pad:
        owned = jnp.pad(owned, ((0, 0), (0, own_pad), (0, 0)))

    nodes = node_flags.shape[1]
    table = jnp.concatenate([node_flags, node_place], axis=0).astype(jnp.bfloat16)
    table = jnp.pad(table, ((0, 14), (0, -nodes % 16)))
    params = pltpu.CompilerParams(vmem_limit_bytes=VMEM)
    pack, ranks = pl.pallas_call(
        functools.partial(prep_kernel, row_devices),
        out_shape=(
            jax.ShapeDtypeStruct((pack_rows, row_count), jnp.bfloat16),
            jax.ShapeDtypeStruct((row_devices, 1, row_count), jnp.float32),
        ),
        compiler_params=params,
    )(targets, bootstrap, node_ids, table)
    gathered = lax.all_gather(pack, "row", axis=0)

    outgoing = pl.pallas_call(
        compact_kernel,
        grid=(row_devices,),
        in_specs=[
            pl.BlockSpec((pack_rows, row_count), lambda d: (0, 0)),
            pl.BlockSpec((feat_count, row_count), lambda d: (0, 0)),
            pl.BlockSpec((1, 1, row_count), lambda d: (d, 0, 0)),
        ],
        out_specs=pl.BlockSpec((1, pack_rows + feat_count, capacity), lambda d: (d, 0, 0)),
        out_shape=jax.ShapeDtypeStruct(
            (row_devices, pack_rows + feat_count, capacity), jnp.bfloat16
        ),
        compiler_params=params,
        cost_estimate=pl.CostEstimate(
            flops=2 * 256 * row_count * row_devices * capacity,
            bytes_accessed=4 * (pack_rows + feat_count) * row_count,
            transcendentals=0,
        ),
    )(pack, features, ranks)
    arrived = lax.all_to_all(outgoing, "row", split_axis=0, concat_axis=0)
    arrived = arrived.reshape(row_devices, pack_rows + feat_count, capacity)
    per_step = row_devices
    if capacity % 128:
        arrived = arrived.transpose(1, 0, 2).reshape(1, -1, row_devices * capacity)
        per_step = 1
    small_gain = node_gains(arrived, arrived, pack_rows, feat_count, 2, width_k, per_step)
    turn = [(g, (g + 1) % leaf_devices) for g in range(leaf_devices)]
    small_gain = lax.ppermute(small_gain, "leaf", turn)[None]

    large_gain = node_gains(gathered, owned, 0, own + own_pad, 1, width_k, 1)[None, :, :own]
    return (large_gain, small_gain)


def solution(mesh):
    placed = (
        P(None, ("dom", "row")),
        P(None, ("dom", "row")),
        P("leaf", ("dom", "row")),
        P("leaf", ("dom", "row")),
        P("leaf", "dom"),
        P("leaf", "dom"),
    )
    return jax.shard_map(
        local,
        mesh=mesh,
        in_specs=placed,
        out_specs=(P("leaf", "dom", "row"), P("leaf", "row", "dom")),
        check_vma=False,
    )
```

```python
import functools

import jax
import jax.numpy as jnp
from jax import lax
from jax.experimental import pallas as pl
from jax.experimental.pallas import tpu as pltpu
from jax.sharding import PartitionSpec as P

B = 64
NL = 4
SB = 4
FB = 16
TAIL = 16
NT = (((1,), (1,)), ((), ()))
VMEM = 50 * 1024 * 1024


def prep_kernel(
    row_devices, targets_ref, boot_ref, ids_ref, table_ref, pack_ref, rank_ref, code_ref=None
):
    width_k, rows = targets_ref.shape
    weight = boot_ref[...].astype(jnp.float32)
    weighted = (targets_ref[...].astype(jnp.float32) * weight).astype(jnp.bfloat16)
    nodes = table_ref.shape[1]
    node_hot = lax.broadcasted_iota(jnp.int32, (nodes, rows), 0) == ids_ref[...]
    node_hot = jnp.where(node_hot, 1.0, 0.0).astype(jnp.bfloat16)
    found = jnp.dot(table_ref[...], node_hot, preferred_element_type=jnp.float32)
    is_large = found[0:1] > 0.5
    place = found[1:2].astype(jnp.int32)
    large_label = jnp.where(is_large, place, NL).astype(jnp.float32)
    slot_label = (place % SB).astype(jnp.float32)
    dest = jnp.where(is_large, row_devices, place // SB)
    tail_row = lax.broadcasted_iota(jnp.int32, (TAIL, rows), 0)
    tail = jnp.where(tail_row == 0, weight, 0.0)
    tail = jnp.where(tail_row == 1, large_label, tail)
    tail = jnp.where(tail_row == 2, slot_label, tail)
    pack_ref[0:width_k, :] = weighted
    pack_ref[width_k : width_k + TAIL, :] = tail.astype(jnp.bfloat16)
    if code_ref is not None:
        code = weight + 4.0 * large_label
        wide = rows // FB
        code = jnp.concatenate(
            [code[:, c * wide : (c + 1) * wide] for c in range(FB)], axis=0
        )
        code_ref[...] = code.astype(jnp.bfloat16)
    dest_rows = rank_ref.shape[0]
    step = 512
    earlier = lax.broadcasted_iota(jnp.int32, (step, step), 0) < lax.broadcasted_iota(
        jnp.int32, (step, step), 1
    )
    earlier = jnp.where(earlier, 1.0, 0.0).astype(jnp.bfloat16)
    carry = jnp.zeros((dest_rows, 1), jnp.float32)
    for at in range(0, rows, step):
        hot = lax.broadcasted_iota(jnp.int32, (dest_rows, step), 0) == dest[:, at : at + step]
        hot_f = jnp.where(hot, 1.0, 0.0)
        before = jnp.dot(hot_f.astype(jnp.bfloat16), earlier, preferred_element_type=jnp.float32)
        ranks = jnp.where(hot, before + carry, -1.0)
        rank_ref[:, 0, at : at + step] = ranks
        carry = carry + jnp.sum(hot_f, axis=1, keepdims=True)


def compact_kernel(pack_ref, features_ref, rank_ref, out_ref):
    rows = features_ref.shape[1]
    capacity = out_ref.shape[2]
    spots = lax.broadcasted_iota(jnp.int32, (capacity, 128), 0).astype(jnp.float32)
    spots = spots.astype(jnp.bfloat16)[:, 0:1]
    ranks = rank_ref[0].astype(jnp.bfloat16)
    hot = jnp.where(spots == ranks, 1.0, 0.0).astype(jnp.bfloat16)
    payload = jnp.concatenate([pack_ref[...], features_ref[...]], axis=0)
    moved = lax.dot_general(payload, hot, NT, preferred_element_type=jnp.float32)
    out_ref[0] = moved.astype(jnp.bfloat16)


def chunk_sums(weighted, weight, label, values):
    step = values.shape[1]
    parts = [weighted * jnp.where(label == n, 1.0, 0.0).astype(jnp.bfloat16) for n in range(NL)]
    node_row = lax.broadcasted_iota(jnp.int32, (TAIL, step), 0).astype(jnp.float32)
    parts.append(jnp.where(node_row == label, weight, 0.0).astype(jnp.bfloat16))
    columns = jnp.concatenate(parts, axis=0)
    one = jnp.ones_like(values)
    zero = jnp.zeros_like(values)
    masks = [
        jnp.where(values < jnp.bfloat16((u - B // 2 + 1) / 16.0), one, zero) for u in range(B - 1)
    ]
    masks.append(one)
    below = jnp.concatenate(masks, axis=0)
    return lax.dot_general(columns, below, NT, preferred_element_type=jnp.float32)


def best_scores(acc_ref, width_k):
    wide = 128
    sums = NL * width_k
    pick = lax.broadcasted_iota(jnp.int32, (wide, wide), 0) == (
        wide - FB + lax.broadcasted_iota(jnp.int32, (wide, wide), 1) % FB
    )
    whole = jnp.dot(
        acc_ref[:, FB * B - wide : FB * B],
        jnp.where(pick, 1.0, 0.0),
        precision=lax.Precision.HIGHEST,
        preferred_element_type=jnp.float32,
    )
    whole_sum = whole[0:sums]
    whole_cnt = whole[sums : sums + 8]

    def term(vec, cnt):
        rows = []
        for n in range(NL):
            part = vec[n * width_k : (n + 1) * width_k]
            rows.append(jnp.sum(part * part, axis=0, keepdims=True))
        return jnp.concatenate(rows, axis=0) / jnp.maximum(cnt[0:NL], 1.0)

    whole_term = term(whole_sum, whole_cnt)
    best = None
    for start in range(0, FB * B, wide):
        left_sum = acc_ref[0:sums, start : start + wide]
        left_cnt = acc_ref[sums : sums + 8, start : start + wide]
        score = term(left_sum, left_cnt) + term(whole_sum - left_sum, whole_cnt - left_cnt)
        score = score - whole_term
        if start == FB * B - wide:
            lane = lax.broadcasted_iota(jnp.int32, (NL, wide), 1)
            score = jnp.where(lane < wide - FB, score, -jnp.inf)
        best = score if best is None else jnp.maximum(best, score)
    return best / width_k


def gain_kernel(width_k, label_row, pack_ref, features_ref, out_ref, acc_ref):
    at = pl.program_id(1)
    sources, _, rows = features_ref.shape
    step = min(rows, 512)

    @pl.when(at == 0)
    def _():
        acc_ref[...] = jnp.zeros_like(acc_ref)

    total = acc_ref[...]
    for source in range(sources):
        for start in range(0, rows, step):
            cut = pl.ds(start, step)
            tail = pack_ref[source, width_k : width_k + TAIL, cut].astype(jnp.float32)
            total = total + chunk_sums(
                pack_ref[source, 0:width_k, cut],
                tail[0:1],
                tail[label_row : label_row + 1],
                features_ref[source, :, cut],
            )
    acc_ref[...] = total

    @pl.when(at == pl.num_programs(1) - 1)
    def _():
        out_ref[0] = best_scores(acc_ref, width_k)


def level_kernel(
    n_row,
    feat_ref,
    targ_ref,
    pack_ref,
    code_ref,
    rank_ref,
    large_ref,
    small_ref,
    owned,
    targs,
    codes,
    payload,
    outgoing,
    arrived,
    acc_ref,
    send_sem,
    recv_sem,
    pass_send,
    pass_recv,
    small_send,
    small_recv,
):
    width_k, rows = targ_ref.shape
    feat_count = feat_ref.shape[0]
    pack_rows = width_k + TAIL
    capacity = outgoing.shape[2]
    me = lax.axis_index("row")
    leaf = lax.axis_index("leaf")
    other = 1 - leaf
    half = rows // 2
    mine = pl.ds(pl.multiple_of(leaf * half, 128), half)

    barrier = pltpu.get_barrier_semaphore()

    def greet(i, _):
        peer = lax.rem(me + i, n_row)
        pl.semaphore_signal(barrier, inc=1, device_id={"row": peer, "leaf": leaf})
        pl.semaphore_signal(barrier, inc=1, device_id={"row": peer, "leaf": other})
        return 0

    lax.fori_loop(1, n_row, greet, 0)
    pl.semaphore_signal(barrier, inc=1, device_id={"row": me, "leaf": other})
    pl.semaphore_wait(barrier, 2 * n_row - 1)

    def first(i):
        peer = lax.rem(me + i, n_row)
        block = pl.ds(pl.multiple_of(peer * FB, FB), FB)
        pairs = (
            (feat_ref.at[block, mine], owned.at[me, :, mine]),
            (targ_ref.at[:, mine], targs.at[me, :, mine]),
            (code_ref, codes.at[me]),
        )
        return [
            pltpu.make_async_remote_copy(
                src_ref=src,
                dst_ref=dst,
                send_sem=send_sem.at[k, i],
                recv_sem=recv_sem.at[k, i],
                device_id={"row": peer, "leaf": leaf},
            )
            for k, (src, dst) in enumerate(pairs)
        ]

    def handed(i):
        source = lax.rem(me - i + n_row, n_row)
        return [
            pltpu.make_async_remote_copy(
                src_ref=buf.at[source, :, mine],
                dst_ref=buf.at[source, :, mine],
                send_sem=pass_send.at[k, i],
                recv_sem=pass_recv.at[k, i],
                device_id={"row": me, "leaf": other},
            )
            for k, buf in enumerate((owned, targs))
        ]

    def small_copy(i):
        peer = lax.rem(me + i, n_row)
        return pltpu.make_async_remote_copy(
            src_ref=outgoing.at[peer],
            dst_ref=arrived.at[me],
            send_sem=small_send.at[i],
            recv_sem=small_recv.at[i],
            device_id={"row": peer, "leaf": other},
        )

    def start_first(i, _):
        for copy in first(i):
            copy.start()
        return 0

    lax.fori_loop(1, n_row, start_first, 0)
    payload[0:pack_rows, :] = pack_ref[...]
    payload[pack_rows : pack_rows + feat_count, :] = feat_ref[...]
    owned[me] = feat_ref[pl.ds(pl.multiple_of(me * FB, FB), FB), :]
    targs[me] = targ_ref[...]
    codes[me] = code_ref[...]
    acc_ref[...] = jnp.zeros_like(acc_ref)

    def compact(i, _):
        peer = lax.rem(me + i, n_row)
        spots = lax.broadcasted_iota(jnp.int32, (capacity, 128), 0).astype(jnp.float32)
        spots = spots.astype(jnp.bfloat16)[:, 0:1]
        ranks = rank_ref[peer].astype(jnp.bfloat16)
        hot = jnp.where(spots == ranks, 1.0, 0.0).astype(jnp.bfloat16)
        moved = lax.dot_general(payload[...], hot, NT, preferred_element_type=jnp.float32)
        outgoing[peer] = moved.astype(jnp.bfloat16)
        small_copy(i).start()
        return 0

    lax.fori_loop(0, n_row, compact, 0)

    def take(i):
        for copy in first(i):
            copy.wait_recv()
        for copy in handed(i):
            copy.start()

    def large(i, _):
        @pl.when(i + 1 < n_row)
        def _():
            take(i + 1)

        @pl.when(i > 0)
        def _():
            for copy in handed(i):
                copy.wait_recv()

        source = lax.rem(me - i + n_row, n_row)
        code = codes[source].astype(jnp.float32)
        code = jnp.concatenate([code[c : c + 1] for c in range(FB)], axis=1)
        label = jnp.floor(code * 0.25)
        weight = code - 4.0 * label
        total = acc_ref[...]
        step = 512
        for start in range(0, rows, step):
            cut = pl.ds(start, step)
            scale = weight[:, start : start + step]
            weighted = (targs[source, :, cut].astype(jnp.float32) * scale).astype(jnp.bfloat16)
            total = total + chunk_sums(
                weighted, scale, label[:, start : start + step], owned[source, :, cut]
            )
        acc_ref[...] = total
        return 0

    lax.fori_loop(0, n_row, large, 0)
    large_ref[...] = best_scores(acc_ref, width_k)

    def small_arrive(i, _):
        small_copy(i).wait_recv()
        return 0

    lax.fori_loop(0, n_row, small_arrive, 0)

    def small(j, _):
        total = jnp.zeros_like(acc_ref)
        block = pl.ds(pl.multiple_of(pack_rows + j * FB, FB), FB)
        for source in range(n_row):
            tail = arrived[source, width_k:pack_rows, :].astype(jnp.float32)
            total = total + chunk_sums(
                arrived[source, 0:width_k, :], tail[0:1], tail[2:3], arrived[source, block, :]
            )
        acc_ref[...] = total
        small_ref[j] = best_scores(acc_ref, width_k)
        return 0

    lax.fori_loop(0, feat_count // FB, small, 0)

    def finish(i, _):
        for copy in first(i) + handed(i):
            copy.wait_send()
        return 0

    lax.fori_loop(1, n_row, finish, 0)

    def finish_small(i, _):
        small_copy(i).wait_send()
        return 0

    lax.fori_loop(0, n_row, finish_small, 0)


def last_bins(best):
    blocks = best.shape[0]
    best = jnp.max(best.reshape(blocks, NL, 128 // FB, FB), axis=2)
    return best.transpose(1, 0, 2).reshape(NL, blocks * FB)


def node_gains(pack, features, feat_row, feat_count, label_row, width_k, per_step):
    sources, pack_rows, rows = pack.shape[0], width_k + TAIL, pack.shape[2]
    blocks = feat_count // FB
    best = pl.pallas_call(
        functools.partial(gain_kernel, width_k, label_row),
        grid=(blocks, sources // per_step),
        in_specs=[
            pl.BlockSpec((per_step, pack_rows, rows), lambda j, i: (i, 0, 0)),
            pl.BlockSpec((per_step, FB, rows), lambda j, i: (i, feat_row // FB + j, 0)),
        ],
        out_specs=pl.BlockSpec((1, NL, 128), lambda j, i: (j, 0, 0)),
        out_shape=jax.ShapeDtypeStruct((blocks, NL, 128), jnp.float32),
        scratch_shapes=[pltpu.VMEM((NL * width_k + TAIL, FB * B), jnp.float32)],
        compiler_params=pltpu.CompilerParams(vmem_limit_bytes=VMEM),
        cost_estimate=pl.CostEstimate(
            flops=2 * feat_count * B * 144 * sources * rows,
            bytes_accessed=2 * sources * rows * (feat_count + 48),
            transcendentals=0,
        ),
    )(pack, features)
    return last_bins(best)


def local(features, targets, bootstrap, node_ids, node_flags, node_place):
    feat_count, row_count = features.shape
    width_k = targets.shape[0]
    row_devices = lax.axis_size("row")
    leaf_devices = lax.axis_size("leaf")
    capacity = row_count // (2 * row_devices)
    own = feat_count // row_devices
    pack_rows = width_k + TAIL

    nodes = node_flags.shape[1]
    table = jnp.concatenate([node_flags, node_place], axis=0).astype(jnp.bfloat16)
    table = jnp.pad(table, ((0, 14), (0, -nodes % 16)))
    params = pltpu.CompilerParams(vmem_limit_bytes=VMEM)
    fused = own == FB and capacity % 128 == 0 and leaf_devices == 2
    shapes = [
        jax.ShapeDtypeStruct((pack_rows, row_count), jnp.bfloat16),
        jax.ShapeDtypeStruct((row_devices, 1, row_count), jnp.float32),
    ]
    if fused:
        shapes.append(jax.ShapeDtypeStruct((FB, row_count // FB), jnp.bfloat16))
    made = pl.pallas_call(
        functools.partial(prep_kernel, row_devices), out_shape=shapes, compiler_params=params
    )(targets, bootstrap, node_ids, table)
    if fused:
        pack, ranks, code = made
        moved = pack_rows + feat_count
        dma = pltpu.SemaphoreType.DMA
        large_best, small_best = pl.pallas_call(
            functools.partial(level_kernel, row_devices),
            out_shape=(
                jax.ShapeDtypeStruct((NL, 128), jnp.float32),
                jax.ShapeDtypeStruct((feat_count // FB, NL, 128), jnp.float32),
            ),
            in_specs=[pl.BlockSpec(memory_space=pltpu.VMEM)] * 5,
            out_specs=(pl.BlockSpec(memory_space=pltpu.VMEM),) * 2,
            scratch_shapes=[
                pltpu.VMEM((row_devices, FB, row_count), jnp.bfloat16),
                pltpu.VMEM((row_devices, width_k, row_count), jnp.bfloat16),
                pltpu.VMEM((row_devices, FB, row_count // FB), jnp.bfloat16),
                pltpu.VMEM((moved, row_count), jnp.bfloat16),
                pltpu.VMEM((row_devices, moved, capacity), jnp.bfloat16),
                pltpu.VMEM((row_devices, moved, capacity), jnp.bfloat16),
                pltpu.VMEM((NL * width_k + TAIL, FB * B), jnp.float32),
                dma((3, row_devices)),
                dma((3, row_devices)),
                dma((2, row_devices)),
                dma((2, row_devices)),
                dma((row_devices,)),
                dma((row_devices,)),
            ],
            compiler_params=pltpu.CompilerParams(
                collective_id=0, has_side_effects=True, vmem_limit_bytes=VMEM
            ),
        )(features, targets, pack, code, ranks)
        return (last_bins(large_best[None])[None], last_bins(small_best)[None])
    pack, ranks = made

    owned = lax.all_to_all(
        features.reshape(row_devices, own, row_count), "row", split_axis=0, concat_axis=0
    )
    owned = owned.reshape(row_devices, own, row_count)
    own_pad = -own % FB
    if own_pad:
        owned = jnp.pad(owned, ((0, 0), (0, own_pad), (0, 0)))

    gathered = lax.all_gather(pack, "row", axis=0)

    outgoing = pl.pallas_call(
        compact_kernel,
        grid=(row_devices,),
        in_specs=[
            pl.BlockSpec((pack_rows, row_count), lambda d: (0, 0)),
            pl.BlockSpec((feat_count, row_count), lambda d: (0, 0)),
            pl.BlockSpec((1, 1, row_count), lambda d: (d, 0, 0)),
        ],
        out_specs=pl.BlockSpec((1, pack_rows + feat_count, capacity), lambda d: (d, 0, 0)),
        out_shape=jax.ShapeDtypeStruct(
            (row_devices, pack_rows + feat_count, capacity), jnp.bfloat16
        ),
        compiler_params=params,
        cost_estimate=pl.CostEstimate(
            flops=2 * 256 * row_count * row_devices * capacity,
            bytes_accessed=4 * (pack_rows + feat_count) * row_count,
            transcendentals=0,
        ),
    )(pack, features, ranks)
    arrived = lax.all_to_all(outgoing, "row", split_axis=0, concat_axis=0)
    arrived = arrived.reshape(row_devices, pack_rows + feat_count, capacity)
    per_step = row_devices
    if capacity % 128:
        arrived = arrived.transpose(1, 0, 2).reshape(1, -1, row_devices * capacity)
        per_step = 1
    small_gain = node_gains(arrived, arrived, pack_rows, feat_count, 2, width_k, per_step)
    turn = [(g, (g + 1) % leaf_devices) for g in range(leaf_devices)]
    small_gain = lax.ppermute(small_gain, "leaf", turn)[None]

    large_gain = node_gains(gathered, owned, 0, own + own_pad, 1, width_k, 1)[None, :, :own]
    return (large_gain, small_gain)


def solution(mesh):
    placed = (
        P(None, ("dom", "row")),
        P(None, ("dom", "row")),
        P("leaf", ("dom", "row")),
        P("leaf", ("dom", "row")),
        P("leaf", "dom"),
        P("leaf", "dom"),
    )
    return jax.shard_map(
        local,
        mesh=mesh,
        in_specs=placed,
        out_specs=(P("leaf", "dom", "row"), P("leaf", "row", "dom")),
        check_vma=False,
    )
```

```python
import functools

import jax
import jax.numpy as jnp
from jax import lax
from jax.experimental import pallas as pl
from jax.experimental.pallas import tpu as pltpu
from jax.sharding import PartitionSpec as P

B = 64
NL = 4
SB = 4
FB = 16
TAIL = 16
NT = (((1,), (1,)), ((), ()))
VMEM = 50 * 1024 * 1024


def prep_kernel(
    row_devices, targets_ref, boot_ref, ids_ref, table_ref, pack_ref, rank_ref, code_ref=None
):
    width_k, rows = targets_ref.shape
    weight = boot_ref[...].astype(jnp.float32)
    weighted = (targets_ref[...].astype(jnp.float32) * weight).astype(jnp.bfloat16)
    nodes = table_ref.shape[1]
    node_hot = lax.broadcasted_iota(jnp.int32, (nodes, rows), 0) == ids_ref[...]
    node_hot = jnp.where(node_hot, 1.0, 0.0).astype(jnp.bfloat16)
    found = jnp.dot(table_ref[...], node_hot, preferred_element_type=jnp.float32)
    is_large = found[0:1] > 0.5
    place = found[1:2].astype(jnp.int32)
    large_label = jnp.where(is_large, place, NL).astype(jnp.float32)
    slot_label = (place % SB).astype(jnp.float32)
    dest = jnp.where(is_large, row_devices, place // SB)
    tail_row = lax.broadcasted_iota(jnp.int32, (TAIL, rows), 0)
    tail = jnp.where(tail_row == 0, weight, 0.0)
    tail = jnp.where(tail_row == 1, large_label, tail)
    tail = jnp.where(tail_row == 2, slot_label, tail)
    pack_ref[0:width_k, :] = weighted
    pack_ref[width_k : width_k + TAIL, :] = tail.astype(jnp.bfloat16)
    if code_ref is not None:
        code = weight + 4.0 * large_label
        wide = rows // FB
        code = jnp.concatenate(
            [code[:, c * wide : (c + 1) * wide] for c in range(FB)], axis=0
        )
        code_ref[...] = code.astype(jnp.bfloat16)
    dest_rows = rank_ref.shape[0]
    step = 512
    earlier = lax.broadcasted_iota(jnp.int32, (step, step), 0) < lax.broadcasted_iota(
        jnp.int32, (step, step), 1
    )
    earlier = jnp.where(earlier, 1.0, 0.0).astype(jnp.bfloat16)
    carry = jnp.zeros((dest_rows, 1), jnp.float32)
    for at in range(0, rows, step):
        hot = lax.broadcasted_iota(jnp.int32, (dest_rows, step), 0) == dest[:, at : at + step]
        hot_f = jnp.where(hot, 1.0, 0.0)
        before = jnp.dot(hot_f.astype(jnp.bfloat16), earlier, preferred_element_type=jnp.float32)
        ranks = jnp.where(hot, before + carry, -1.0)
        rank_ref[:, 0, at : at + step] = ranks
        carry = carry + jnp.sum(hot_f, axis=1, keepdims=True)


def compact_kernel(pack_ref, features_ref, rank_ref, out_ref):
    rows = features_ref.shape[1]
    capacity = out_ref.shape[2]
    spots = lax.broadcasted_iota(jnp.int32, (capacity, 128), 0).astype(jnp.float32)
    spots = spots.astype(jnp.bfloat16)[:, 0:1]
    ranks = rank_ref[0].astype(jnp.bfloat16)
    hot = jnp.where(spots == ranks, 1.0, 0.0).astype(jnp.bfloat16)
    payload = jnp.concatenate([pack_ref[...], features_ref[...]], axis=0)
    moved = lax.dot_general(payload, hot, NT, preferred_element_type=jnp.float32)
    out_ref[0] = moved.astype(jnp.bfloat16)


def chunk_sums(weighted, weight, label, values):
    step = values.shape[1]
    parts = [weighted * jnp.where(label == n, 1.0, 0.0).astype(jnp.bfloat16) for n in range(NL)]
    node_row = lax.broadcasted_iota(jnp.int32, (TAIL, step), 0).astype(jnp.float32)
    parts.append(jnp.where(node_row == label, weight, 0.0).astype(jnp.bfloat16))
    columns = jnp.concatenate(parts, axis=0)
    tall = jnp.concatenate([values] * (128 // FB), axis=0).T
    one = jnp.ones_like(tall)
    zero = jnp.zeros_like(tall)
    bins = lax.broadcasted_iota(jnp.int32, (1, 128), 1) // FB
    masks = []
    for first in range(0, B, 128 // FB):
        u = bins + first
        edge = (u - (B // 2 - 1)).astype(jnp.float32) / 16.0
        edge = jnp.where(u == B - 1, jnp.inf, edge).astype(jnp.bfloat16)
        masks.append(jnp.where(tall < edge, one, zero))
    below = jnp.concatenate(masks, axis=1)
    return jnp.dot(columns, below, preferred_element_type=jnp.float32)


def best_scores(acc_ref, width_k):
    wide = 128
    sums = NL * width_k
    pick = lax.broadcasted_iota(jnp.int32, (wide, wide), 0) == (
        wide - FB + lax.broadcasted_iota(jnp.int32, (wide, wide), 1) % FB
    )
    whole = jnp.dot(
        acc_ref[:, FB * B - wide : FB * B],
        jnp.where(pick, 1.0, 0.0),
        precision=lax.Precision.HIGHEST,
        preferred_element_type=jnp.float32,
    )
    whole_sum = whole[0:sums]
    whole_cnt = whole[sums : sums + 8]

    def term(vec, cnt):
        rows = []
        for n in range(NL):
            part = vec[n * width_k : (n + 1) * width_k]
            rows.append(jnp.sum(part * part, axis=0, keepdims=True))
        return jnp.concatenate(rows, axis=0) / jnp.maximum(cnt[0:NL], 1.0)

    whole_term = term(whole_sum, whole_cnt)
    best = None
    for start in range(0, FB * B, wide):
        left_sum = acc_ref[0:sums, start : start + wide]
        left_cnt = acc_ref[sums : sums + 8, start : start + wide]
        score = term(left_sum, left_cnt) + term(whole_sum - left_sum, whole_cnt - left_cnt)
        score = score - whole_term
        if start == FB * B - wide:
            lane = lax.broadcasted_iota(jnp.int32, (NL, wide), 1)
            score = jnp.where(lane < wide - FB, score, -jnp.inf)
        best = score if best is None else jnp.maximum(best, score)
    return best / width_k


def gain_kernel(width_k, label_row, pack_ref, features_ref, out_ref, acc_ref):
    at = pl.program_id(1)
    sources, _, rows = features_ref.shape
    step = min(rows, 512)

    @pl.when(at == 0)
    def _():
        acc_ref[...] = jnp.zeros_like(acc_ref)

    total = acc_ref[...]
    for source in range(sources):
        for start in range(0, rows, step):
            cut = pl.ds(start, step)
            tail = pack_ref[source, width_k : width_k + TAIL, cut].astype(jnp.float32)
            total = total + chunk_sums(
                pack_ref[source, 0:width_k, cut],
                tail[0:1],
                tail[label_row : label_row + 1],
                features_ref[source, :, cut],
            )
    acc_ref[...] = total

    @pl.when(at == pl.num_programs(1) - 1)
    def _():
        out_ref[0] = best_scores(acc_ref, width_k)


def level_kernel(
    n_row,
    feat_ref,
    targ_ref,
    pack_ref,
    code_ref,
    rank_ref,
    large_ref,
    small_ref,
    owned,
    targs,
    codes,
    payload,
    outgoing,
    arrived,
    acc_ref,
    send_sem,
    recv_sem,
    pass_send,
    pass_recv,
    small_send,
    small_recv,
):
    width_k, rows = targ_ref.shape
    feat_count = feat_ref.shape[0]
    pack_rows = width_k + TAIL
    capacity = outgoing.shape[2]
    me = lax.axis_index("row")
    leaf = lax.axis_index("leaf")
    other = 1 - leaf
    half = rows // 2
    mine = pl.ds(pl.multiple_of(leaf * half, 128), half)

    barrier = pltpu.get_barrier_semaphore()

    def greet(i, _):
        peer = lax.rem(me + i, n_row)
        pl.semaphore_signal(barrier, inc=1, device_id={"row": peer, "leaf": leaf})
        pl.semaphore_signal(barrier, inc=1, device_id={"row": peer, "leaf": other})
        return 0

    lax.fori_loop(1, n_row, greet, 0)
    pl.semaphore_signal(barrier, inc=1, device_id={"row": me, "leaf": other})
    pl.semaphore_wait(barrier, 2 * n_row - 1)

    def first(i):
        peer = lax.rem(me + i, n_row)
        block = pl.ds(pl.multiple_of(peer * FB, FB), FB)
        pairs = (
            (feat_ref.at[block, mine], owned.at[me, :, mine]),
            (targ_ref.at[:, mine], targs.at[me, :, mine]),
            (code_ref, codes.at[me]),
        )
        return [
            pltpu.make_async_remote_copy(
                src_ref=src,
                dst_ref=dst,
                send_sem=send_sem.at[k, i],
                recv_sem=recv_sem.at[k, i],
                device_id={"row": peer, "leaf": leaf},
            )
            for k, (src, dst) in enumerate(pairs)
        ]

    def handed(i):
        source = lax.rem(me - i + n_row, n_row)
        return [
            pltpu.make_async_remote_copy(
                src_ref=buf.at[source, :, mine],
                dst_ref=buf.at[source, :, mine],
                send_sem=pass_send.at[k, i],
                recv_sem=pass_recv.at[k, i],
                device_id={"row": me, "leaf": other},
            )
            for k, buf in enumerate((owned, targs))
        ]

    def small_copy(i):
        peer = lax.rem(me + i, n_row)
        return pltpu.make_async_remote_copy(
            src_ref=outgoing.at[peer],
            dst_ref=arrived.at[me],
            send_sem=small_send.at[i],
            recv_sem=small_recv.at[i],
            device_id={"row": peer, "leaf": other},
        )

    def start_first(i, _):
        for copy in first(i):
            copy.start()
        return 0

    lax.fori_loop(1, n_row, start_first, 0)
    payload[0:pack_rows, :] = pack_ref[...]
    payload[pack_rows : pack_rows + feat_count, :] = feat_ref[...]
    owned[me] = feat_ref[pl.ds(pl.multiple_of(me * FB, FB), FB), :]
    targs[me] = targ_ref[...]
    codes[me] = code_ref[...]
    acc_ref[...] = jnp.zeros_like(acc_ref)

    def compact(i, _):
        peer = lax.rem(me + i, n_row)
        lane = lax.broadcasted_iota(jnp.int32, (1, 128), 1).astype(jnp.float32)
        moved = jnp.zeros((pack_rows + feat_count, capacity), jnp.float32)
        step = 512
        for at in range(0, rows, step):
            ranks = rank_ref[peer, :, at : at + step].astype(jnp.bfloat16)
            tall = jnp.broadcast_to(ranks, (128, step)).T
            hot = [
                jnp.where(tall == (lane + c).astype(jnp.bfloat16), 1.0, 0.0).astype(jnp.bfloat16)
                for c in range(0, capacity, 128)
            ]
            moved = moved + jnp.dot(
                payload[:, at : at + step],
                jnp.concatenate(hot, axis=1),
                preferred_element_type=jnp.float32,
            )
        outgoing[peer] = moved.astype(jnp.bfloat16)
        small_copy(i).start()
        return 0

    lax.fori_loop(0, n_row, compact, 0)

    def take(i):
        for copy in first(i):
            copy.wait_recv()
        for copy in handed(i):
            copy.start()

    def large(i, _):
        @pl.when(i + 1 < n_row)
        def _():
            take(i + 1)

        @pl.when(i > 0)
        def _():
            for copy in handed(i):
                copy.wait_recv()

        source = lax.rem(me - i + n_row, n_row)
        code = codes[source].astype(jnp.float32)
        code = jnp.concatenate([code[c : c + 1] for c in range(FB)], axis=1)
        label = jnp.floor(code * 0.25)
        weight = code - 4.0 * label
        total = acc_ref[...]
        step = 512
        for start in range(0, rows, step):
            cut = pl.ds(start, step)
            scale = weight[:, start : start + step]
            weighted = (targs[source, :, cut].astype(jnp.float32) * scale).astype(jnp.bfloat16)
            total = total + chunk_sums(
                weighted, scale, label[:, start : start + step], owned[source, :, cut]
            )
        acc_ref[...] = total
        return 0

    lax.fori_loop(0, n_row, large, 0)
    large_ref[...] = best_scores(acc_ref, width_k)

    def small_arrive(i, _):
        small_copy(i).wait_recv()
        return 0

    lax.fori_loop(0, n_row, small_arrive, 0)

    def small(j, _):
        total = jnp.zeros_like(acc_ref)
        block = pl.ds(pl.multiple_of(pack_rows + j * FB, FB), FB)
        for source in range(n_row):
            tail = arrived[source, width_k:pack_rows, :].astype(jnp.float32)
            total = total + chunk_sums(
                arrived[source, 0:width_k, :], tail[0:1], tail[2:3], arrived[source, block, :]
            )
        acc_ref[...] = total
        small_ref[j] = best_scores(acc_ref, width_k)
        return 0

    lax.fori_loop(0, feat_count // FB, small, 0)

    def finish(i, _):
        for copy in first(i) + handed(i):
            copy.wait_send()
        return 0

    lax.fori_loop(1, n_row, finish, 0)

    def finish_small(i, _):
        small_copy(i).wait_send()
        return 0

    lax.fori_loop(0, n_row, finish_small, 0)


def last_bins(best):
    blocks = best.shape[0]
    best = jnp.max(best.reshape(blocks, NL, 128 // FB, FB), axis=2)
    return best.transpose(1, 0, 2).reshape(NL, blocks * FB)


def node_gains(pack, features, feat_row, feat_count, label_row, width_k, per_step):
    sources, pack_rows, rows = pack.shape[0], width_k + TAIL, pack.shape[2]
    blocks = feat_count // FB
    best = pl.pallas_call(
        functools.partial(gain_kernel, width_k, label_row),
        grid=(blocks, sources // per_step),
        in_specs=[
            pl.BlockSpec((per_step, pack_rows, rows), lambda j, i: (i, 0, 0)),
            pl.BlockSpec((per_step, FB, rows), lambda j, i: (i, feat_row // FB + j, 0)),
        ],
        out_specs=pl.BlockSpec((1, NL, 128), lambda j, i: (j, 0, 0)),
        out_shape=jax.ShapeDtypeStruct((blocks, NL, 128), jnp.float32),
        scratch_shapes=[pltpu.VMEM((NL * width_k + TAIL, FB * B), jnp.float32)],
        compiler_params=pltpu.CompilerParams(vmem_limit_bytes=VMEM),
        cost_estimate=pl.CostEstimate(
            flops=2 * feat_count * B * 144 * sources * rows,
            bytes_accessed=2 * sources * rows * (feat_count + 48),
            transcendentals=0,
        ),
    )(pack, features)
    return last_bins(best)


def local(features, targets, bootstrap, node_ids, node_flags, node_place):
    feat_count, row_count = features.shape
    width_k = targets.shape[0]
    row_devices = lax.axis_size("row")
    leaf_devices = lax.axis_size("leaf")
    capacity = row_count // (2 * row_devices)
    own = feat_count // row_devices
    pack_rows = width_k + TAIL

    nodes = node_flags.shape[1]
    table = jnp.concatenate([node_flags, node_place], axis=0).astype(jnp.bfloat16)
    table = jnp.pad(table, ((0, 14), (0, -nodes % 16)))
    params = pltpu.CompilerParams(vmem_limit_bytes=VMEM)
    fused = own == FB and capacity % 128 == 0 and leaf_devices == 2
    shapes = [
        jax.ShapeDtypeStruct((pack_rows, row_count), jnp.bfloat16),
        jax.ShapeDtypeStruct((row_devices, 1, row_count), jnp.float32),
    ]
    if fused:
        shapes.append(jax.ShapeDtypeStruct((FB, row_count // FB), jnp.bfloat16))
    made = pl.pallas_call(
        functools.partial(prep_kernel, row_devices), out_shape=shapes, compiler_params=params
    )(targets, bootstrap, node_ids, table)
    if fused:
        pack, ranks, code = made
        moved = pack_rows + feat_count
        dma = pltpu.SemaphoreType.DMA
        large_best, small_best = pl.pallas_call(
            functools.partial(level_kernel, row_devices),
            out_shape=(
                jax.ShapeDtypeStruct((NL, 128), jnp.float32),
                jax.ShapeDtypeStruct((feat_count // FB, NL, 128), jnp.float32),
            ),
            in_specs=[pl.BlockSpec(memory_space=pltpu.VMEM)] * 5,
            out_specs=(pl.BlockSpec(memory_space=pltpu.VMEM),) * 2,
            scratch_shapes=[
                pltpu.VMEM((row_devices, FB, row_count), jnp.bfloat16),
                pltpu.VMEM((row_devices, width_k, row_count), jnp.bfloat16),
                pltpu.VMEM((row_devices, FB, row_count // FB), jnp.bfloat16),
                pltpu.VMEM((moved, row_count), jnp.bfloat16),
                pltpu.VMEM((row_devices, moved, capacity), jnp.bfloat16),
                pltpu.VMEM((row_devices, moved, capacity), jnp.bfloat16),
                pltpu.VMEM((NL * width_k + TAIL, FB * B), jnp.float32),
                dma((3, row_devices)),
                dma((3, row_devices)),
                dma((2, row_devices)),
                dma((2, row_devices)),
                dma((row_devices,)),
                dma((row_devices,)),
            ],
            compiler_params=pltpu.CompilerParams(
                collective_id=0, has_side_effects=True, vmem_limit_bytes=VMEM
            ),
        )(features, targets, pack, code, ranks)
        return (last_bins(large_best[None])[None], last_bins(small_best)[None])
    pack, ranks = made

    owned = lax.all_to_all(
        features.reshape(row_devices, own, row_count), "row", split_axis=0, concat_axis=0
    )
    owned = owned.reshape(row_devices, own, row_count)
    own_pad = -own % FB
    if own_pad:
        owned = jnp.pad(owned, ((0, 0), (0, own_pad), (0, 0)))

    gathered = lax.all_gather(pack, "row", axis=0)

    outgoing = pl.pallas_call(
        compact_kernel,
        grid=(row_devices,),
        in_specs=[
            pl.BlockSpec((pack_rows, row_count), lambda d: (0, 0)),
            pl.BlockSpec((feat_count, row_count), lambda d: (0, 0)),
            pl.BlockSpec((1, 1, row_count), lambda d: (d, 0, 0)),
        ],
        out_specs=pl.BlockSpec((1, pack_rows + feat_count, capacity), lambda d: (d, 0, 0)),
        out_shape=jax.ShapeDtypeStruct(
            (row_devices, pack_rows + feat_count, capacity), jnp.bfloat16
        ),
        compiler_params=params,
        cost_estimate=pl.CostEstimate(
            flops=2 * 256 * row_count * row_devices * capacity,
            bytes_accessed=4 * (pack_rows + feat_count) * row_count,
            transcendentals=0,
        ),
    )(pack, features, ranks)
    arrived = lax.all_to_all(outgoing, "row", split_axis=0, concat_axis=0)
    arrived = arrived.reshape(row_devices, pack_rows + feat_count, capacity)
    per_step = row_devices
    if capacity % 128:
        arrived = arrived.transpose(1, 0, 2).reshape(1, -1, row_devices * capacity)
        per_step = 1
    small_gain = node_gains(arrived, arrived, pack_rows, feat_count, 2, width_k, per_step)
    turn = [(g, (g + 1) % leaf_devices) for g in range(leaf_devices)]
    small_gain = lax.ppermute(small_gain, "leaf", turn)[None]

    large_gain = node_gains(gathered, owned, 0, own + own_pad, 1, width_k, 1)[None, :, :own]
    return (large_gain, small_gain)


def solution(mesh):
    placed = (
        P(None, ("dom", "row")),
        P(None, ("dom", "row")),
        P("leaf", ("dom", "row")),
        P("leaf", ("dom", "row")),
        P("leaf", "dom"),
        P("leaf", "dom"),
    )
    return jax.shard_map(
        local,
        mesh=mesh,
        in_specs=placed,
        out_specs=(P("leaf", "dom", "row"), P("leaf", "row", "dom")),
        check_vma=False,
    )
```

```python
import functools

import jax
import jax.numpy as jnp
from jax import lax
from jax.experimental import pallas as pl
from jax.experimental.pallas import tpu as pltpu
from jax.sharding import PartitionSpec as P

B = 64
NL = 4
SB = 4
FB = 16
TAIL = 16
NT = (((1,), (1,)), ((), ()))
VMEM = 50 * 1024 * 1024


def prep_kernel(
    row_devices, targets_ref, boot_ref, ids_ref, table_ref, pack_ref, rank_ref, code_ref=None
):
    width_k, rows = targets_ref.shape
    weight = boot_ref[...].astype(jnp.float32)
    weighted = (targets_ref[...].astype(jnp.float32) * weight).astype(jnp.bfloat16)
    nodes = table_ref.shape[1]
    node_hot = lax.broadcasted_iota(jnp.int32, (nodes, rows), 0) == ids_ref[...]
    node_hot = jnp.where(node_hot, 1.0, 0.0).astype(jnp.bfloat16)
    found = jnp.dot(table_ref[...], node_hot, preferred_element_type=jnp.float32)
    is_large = found[0:1] > 0.5
    place = found[1:2].astype(jnp.int32)
    large_label = jnp.where(is_large, place, NL).astype(jnp.float32)
    slot_label = (place % SB).astype(jnp.float32)
    dest = jnp.where(is_large, row_devices, place // SB)
    tail_row = lax.broadcasted_iota(jnp.int32, (TAIL, rows), 0)
    tail = jnp.where(tail_row == 0, weight, 0.0)
    tail = jnp.where(tail_row == 1, large_label, tail)
    tail = jnp.where(tail_row == 2, slot_label, tail)
    pack_ref[0:width_k, :] = weighted
    pack_ref[width_k : width_k + TAIL, :] = tail.astype(jnp.bfloat16)
    if code_ref is not None:
        code = weight + 4.0 * large_label
        wide = rows // FB
        code = jnp.concatenate(
            [code[:, c * wide : (c + 1) * wide] for c in range(FB)], axis=0
        )
        code_ref[...] = code.astype(jnp.bfloat16)
    dest_rows = rank_ref.shape[0]
    step = 512
    earlier = lax.broadcasted_iota(jnp.int32, (step, step), 0) < lax.broadcasted_iota(
        jnp.int32, (step, step), 1
    )
    earlier = jnp.where(earlier, 1.0, 0.0).astype(jnp.bfloat16)
    carry = jnp.zeros((dest_rows, 1), jnp.float32)
    for at in range(0, rows, step):
        hot = lax.broadcasted_iota(jnp.int32, (dest_rows, step), 0) == dest[:, at : at + step]
        hot_f = jnp.where(hot, 1.0, 0.0)
        before = jnp.dot(hot_f.astype(jnp.bfloat16), earlier, preferred_element_type=jnp.float32)
        ranks = jnp.where(hot, before + carry, -1.0)
        rank_ref[:, 0, at : at + step] = ranks
        carry = carry + jnp.sum(hot_f, axis=1, keepdims=True)


def compact_kernel(pack_ref, features_ref, rank_ref, out_ref):
    rows = features_ref.shape[1]
    capacity = out_ref.shape[2]
    spots = lax.broadcasted_iota(jnp.int32, (capacity, 128), 0).astype(jnp.float32)
    spots = spots.astype(jnp.bfloat16)[:, 0:1]
    ranks = rank_ref[0].astype(jnp.bfloat16)
    hot = jnp.where(spots == ranks, 1.0, 0.0).astype(jnp.bfloat16)
    payload = jnp.concatenate([pack_ref[...], features_ref[...]], axis=0)
    moved = lax.dot_general(payload, hot, NT, preferred_element_type=jnp.float32)
    out_ref[0] = moved.astype(jnp.bfloat16)


def chunk_sums(weighted, weight, label, values):
    step = values.shape[1]
    parts = [weighted * jnp.where(label == n, 1.0, 0.0).astype(jnp.bfloat16) for n in range(NL)]
    node_row = lax.broadcasted_iota(jnp.int32, (TAIL, step), 0).astype(jnp.float32)
    parts.append(jnp.where(node_row == label, weight, 0.0).astype(jnp.bfloat16))
    columns = jnp.concatenate(parts, axis=0)
    tall = jnp.concatenate([values] * (128 // FB), axis=0).T
    one = jnp.ones_like(tall)
    zero = jnp.zeros_like(tall)
    bins = lax.broadcasted_iota(jnp.int32, (1, 128), 1) // FB
    masks = []
    for first in range(0, B, 128 // FB):
        u = bins + first
        edge = (u - (B // 2 - 1)).astype(jnp.float32) / 16.0
        edge = jnp.where(u == B - 1, jnp.inf, edge).astype(jnp.bfloat16)
        masks.append(jnp.where(tall < edge, one, zero))
    below = jnp.concatenate(masks, axis=1)
    return jnp.dot(columns, below, preferred_element_type=jnp.float32)


def best_scores(acc_ref, width_k):
    wide = 128
    sums = NL * width_k
    pick = lax.broadcasted_iota(jnp.int32, (wide, wide), 0) == (
        wide - FB + lax.broadcasted_iota(jnp.int32, (wide, wide), 1) % FB
    )
    whole = jnp.dot(
        acc_ref[:, FB * B - wide : FB * B],
        jnp.where(pick, 1.0, 0.0),
        precision=lax.Precision.HIGHEST,
        preferred_element_type=jnp.float32,
    )
    whole_sum = whole[0:sums]
    whole_cnt = whole[sums : sums + 8]

    def term(vec, cnt):
        rows = []
        for n in range(NL):
            part = vec[n * width_k : (n + 1) * width_k]
            rows.append(jnp.sum(part * part, axis=0, keepdims=True))
        return jnp.concatenate(rows, axis=0) / jnp.maximum(cnt[0:NL], 1.0)

    whole_term = term(whole_sum, whole_cnt)
    best = None
    for start in range(0, FB * B, wide):
        left_sum = acc_ref[0:sums, start : start + wide]
        left_cnt = acc_ref[sums : sums + 8, start : start + wide]
        score = term(left_sum, left_cnt) + term(whole_sum - left_sum, whole_cnt - left_cnt)
        score = score - whole_term
        if start == FB * B - wide:
            lane = lax.broadcasted_iota(jnp.int32, (NL, wide), 1)
            score = jnp.where(lane < wide - FB, score, -jnp.inf)
        best = score if best is None else jnp.maximum(best, score)
    return best / width_k


def gain_kernel(width_k, label_row, pack_ref, features_ref, out_ref, acc_ref):
    at = pl.program_id(1)
    sources, _, rows = features_ref.shape
    step = min(rows, 512)

    @pl.when(at == 0)
    def _():
        acc_ref[...] = jnp.zeros_like(acc_ref)

    total = acc_ref[...]
    for source in range(sources):
        for start in range(0, rows, step):
            cut = pl.ds(start, step)
            tail = pack_ref[source, width_k : width_k + TAIL, cut].astype(jnp.float32)
            total = total + chunk_sums(
                pack_ref[source, 0:width_k, cut],
                tail[0:1],
                tail[label_row : label_row + 1],
                features_ref[source, :, cut],
            )
    acc_ref[...] = total

    @pl.when(at == pl.num_programs(1) - 1)
    def _():
        out_ref[0] = best_scores(acc_ref, width_k)


def flipped(index, mask, count):
    out, bit = 0, 1
    while bit < count:
        out = out + bit * lax.rem(index // bit + mask // bit, 2)
        bit *= 2
    return out


def level_kernel(
    n_row,
    feat_ref,
    targ_ref,
    pack_ref,
    code_ref,
    rank_ref,
    large_ref,
    small_ref,
    owned,
    targs,
    codes,
    payload,
    outgoing,
    arrived,
    acc_ref,
    send_sem,
    recv_sem,
    pass_send,
    pass_recv,
    small_send,
    small_recv,
):
    width_k, rows = targ_ref.shape
    feat_count = feat_ref.shape[0]
    pack_rows = width_k + TAIL
    capacity = outgoing.shape[2]
    me = lax.axis_index("row")
    leaf = lax.axis_index("leaf")
    other = 1 - leaf
    half = rows // 2
    mine = pl.ds(pl.multiple_of(leaf * half, 128), half)

    barrier = pltpu.get_barrier_semaphore()

    def greet(i, _):
        peer = lax.rem(me + i, n_row)
        pl.semaphore_signal(barrier, inc=1, device_id={"row": peer, "leaf": leaf})
        pl.semaphore_signal(barrier, inc=1, device_id={"row": peer, "leaf": other})
        return 0

    lax.fori_loop(1, n_row, greet, 0)
    pl.semaphore_signal(barrier, inc=1, device_id={"row": me, "leaf": other})
    pl.semaphore_wait(barrier, 2 * n_row - 1)

    def first(i):
        peer = flipped(me, i, n_row)
        block = pl.ds(pl.multiple_of(peer * FB, FB), FB)
        pairs = (
            (feat_ref.at[block, mine], owned.at[me, :, mine]),
            (targ_ref.at[:, mine], targs.at[me, :, mine]),
            (code_ref, codes.at[me]),
        )
        return [
            pltpu.make_async_remote_copy(
                src_ref=src,
                dst_ref=dst,
                send_sem=send_sem.at[k, i],
                recv_sem=recv_sem.at[k, i],
                device_id={"row": peer, "leaf": leaf},
            )
            for k, (src, dst) in enumerate(pairs)
        ]

    def handed(i):
        source = flipped(me, i, n_row)
        return [
            pltpu.make_async_remote_copy(
                src_ref=buf.at[source, :, mine],
                dst_ref=buf.at[source, :, mine],
                send_sem=pass_send.at[k, i],
                recv_sem=pass_recv.at[k, i],
                device_id={"row": me, "leaf": other},
            )
            for k, buf in enumerate((owned, targs))
        ]

    def passed(i):
        source = flipped(me, i, n_row)
        return pltpu.make_async_remote_copy(
            src_ref=targs.at[source, :, mine],
            dst_ref=targs.at[source, :, mine],
            send_sem=send_sem.at[1, i + 1],
            recv_sem=recv_sem.at[1, i + 1],
            device_id={"row": flipped(me, 1, n_row), "leaf": leaf},
        )

    def small_copy(i):
        peer = lax.rem(me + i, n_row)
        return pltpu.make_async_remote_copy(
            src_ref=outgoing.at[peer],
            dst_ref=arrived.at[me],
            send_sem=small_send.at[i],
            recv_sem=small_recv.at[i],
            device_id={"row": peer, "leaf": other},
        )

    def start_even(p, _):
        for copy in first(2 * p):
            copy.start()
        return 0

    lax.fori_loop(1, n_row // 2, start_even, 0)
    for copy in first(1):
        copy.start()

    def start_odd(p, _):
        feature_copy, _, code_copy = first(2 * p + 1)
        feature_copy.start()
        code_copy.start()
        return 0

    lax.fori_loop(1, n_row // 2, start_odd, 0)
    payload[0:pack_rows, :] = pack_ref[...]
    payload[pack_rows : pack_rows + feat_count, :] = feat_ref[...]
    owned[me] = feat_ref[pl.ds(pl.multiple_of(me * FB, FB), FB), :]
    targs[me] = targ_ref[...]
    codes[me] = code_ref[...]
    acc_ref[...] = jnp.zeros_like(acc_ref)

    def compact(i, _):
        peer = lax.rem(me + i, n_row)
        lane = lax.broadcasted_iota(jnp.int32, (1, 128), 1).astype(jnp.float32)
        moved = jnp.zeros((pack_rows + feat_count, capacity), jnp.float32)
        step = 512
        for at in range(0, rows, step):
            ranks = rank_ref[peer, :, at : at + step].astype(jnp.bfloat16)
            tall = jnp.broadcast_to(ranks, (128, step)).T
            hot = [
                jnp.where(tall == (lane + c).astype(jnp.bfloat16), 1.0, 0.0).astype(jnp.bfloat16)
                for c in range(0, capacity, 128)
            ]
            moved = moved + jnp.dot(
                payload[:, at : at + step],
                jnp.concatenate(hot, axis=1),
                preferred_element_type=jnp.float32,
            )
        outgoing[peer] = moved.astype(jnp.bfloat16)
        small_copy(i).start()
        return 0

    lax.fori_loop(0, n_row, compact, 0)

    def take(i):
        for copy in first(i):
            copy.wait_recv()
        for copy in handed(i):
            copy.start()

        @pl.when(i % 2 == 0)
        def _():
            passed(i).start()

    def order(p):
        return (2 * p) % n_row + (2 * p) // n_row

    def large(p, _):
        i = order(p)

        @pl.when(p + 1 < n_row)
        def _():
            take(order(p + 1))

        @pl.when(i > 0)
        def _():
            for copy in handed(i):
                copy.wait_recv()

        source = flipped(me, i, n_row)
        code = codes[source].astype(jnp.float32)
        code = jnp.concatenate([code[c : c + 1] for c in range(FB)], axis=1)
        label = jnp.floor(code * 0.25)
        weight = code - 4.0 * label
        total = acc_ref[...]
        step = 512
        for start in range(0, rows, step):
            cut = pl.ds(start, step)
            scale = weight[:, start : start + step]
            weighted = (targs[source, :, cut].astype(jnp.float32) * scale).astype(jnp.bfloat16)
            total = total + chunk_sums(
                weighted, scale, label[:, start : start + step], owned[source, :, cut]
            )
        acc_ref[...] = total
        return 0

    lax.fori_loop(0, n_row, large, 0)
    large_ref[...] = best_scores(acc_ref, width_k)

    def small_arrive(i, _):
        small_copy(i).wait_recv()
        return 0

    lax.fori_loop(0, n_row, small_arrive, 0)

    def small(j, _):
        total = jnp.zeros_like(acc_ref)
        block = pl.ds(pl.multiple_of(pack_rows + j * FB, FB), FB)
        for source in range(n_row):
            tail = arrived[source, width_k:pack_rows, :].astype(jnp.float32)
            total = total + chunk_sums(
                arrived[source, 0:width_k, :], tail[0:1], tail[2:3], arrived[source, block, :]
            )
        acc_ref[...] = total
        small_ref[j] = best_scores(acc_ref, width_k)
        return 0

    lax.fori_loop(0, feat_count // FB, small, 0)

    def finish(i, _):
        for copy in first(i) + handed(i):
            copy.wait_send()
        return 0

    lax.fori_loop(1, n_row, finish, 0)

    def finish_small(i, _):
        small_copy(i).wait_send()
        return 0

    lax.fori_loop(0, n_row, finish_small, 0)


def last_bins(best):
    blocks = best.shape[0]
    best = jnp.max(best.reshape(blocks, NL, 128 // FB, FB), axis=2)
    return best.transpose(1, 0, 2).reshape(NL, blocks * FB)


def node_gains(pack, features, feat_row, feat_count, label_row, width_k, per_step):
    sources, pack_rows, rows = pack.shape[0], width_k + TAIL, pack.shape[2]
    blocks = feat_count // FB
    best = pl.pallas_call(
        functools.partial(gain_kernel, width_k, label_row),
        grid=(blocks, sources // per_step),
        in_specs=[
            pl.BlockSpec((per_step, pack_rows, rows), lambda j, i: (i, 0, 0)),
            pl.BlockSpec((per_step, FB, rows), lambda j, i: (i, feat_row // FB + j, 0)),
        ],
        out_specs=pl.BlockSpec((1, NL, 128), lambda j, i: (j, 0, 0)),
        out_shape=jax.ShapeDtypeStruct((blocks, NL, 128), jnp.float32),
        scratch_shapes=[pltpu.VMEM((NL * width_k + TAIL, FB * B), jnp.float32)],
        compiler_params=pltpu.CompilerParams(vmem_limit_bytes=VMEM),
        cost_estimate=pl.CostEstimate(
            flops=2 * feat_count * B * 144 * sources * rows,
            bytes_accessed=2 * sources * rows * (feat_count + 48),
            transcendentals=0,
        ),
    )(pack, features)
    return last_bins(best)


def local(features, targets, bootstrap, node_ids, node_flags, node_place):
    feat_count, row_count = features.shape
    width_k = targets.shape[0]
    row_devices = lax.axis_size("row")
    leaf_devices = lax.axis_size("leaf")
    capacity = row_count // (2 * row_devices)
    own = feat_count // row_devices
    pack_rows = width_k + TAIL

    nodes = node_flags.shape[1]
    table = jnp.concatenate([node_flags, node_place], axis=0).astype(jnp.bfloat16)
    table = jnp.pad(table, ((0, 14), (0, -nodes % 16)))
    params = pltpu.CompilerParams(vmem_limit_bytes=VMEM)
    fused = own == FB and capacity % 128 == 0 and leaf_devices == 2
    fused = fused and row_devices >= 4 and row_devices & (row_devices - 1) == 0
    shapes = [
        jax.ShapeDtypeStruct((pack_rows, row_count), jnp.bfloat16),
        jax.ShapeDtypeStruct((row_devices, 1, row_count), jnp.float32),
    ]
    if fused:
        shapes.append(jax.ShapeDtypeStruct((FB, row_count // FB), jnp.bfloat16))
    made = pl.pallas_call(
        functools.partial(prep_kernel, row_devices), out_shape=shapes, compiler_params=params
    )(targets, bootstrap, node_ids, table)
    if fused:
        pack, ranks, code = made
        moved = pack_rows + feat_count
        dma = pltpu.SemaphoreType.DMA
        large_best, small_best = pl.pallas_call(
            functools.partial(level_kernel, row_devices),
            out_shape=(
                jax.ShapeDtypeStruct((NL, 128), jnp.float32),
                jax.ShapeDtypeStruct((feat_count // FB, NL, 128), jnp.float32),
            ),
            in_specs=[pl.BlockSpec(memory_space=pltpu.VMEM)] * 5,
            out_specs=(pl.BlockSpec(memory_space=pltpu.VMEM),) * 2,
            scratch_shapes=[
                pltpu.VMEM((row_devices, FB, row_count), jnp.bfloat16),
                pltpu.VMEM((row_devices, width_k, row_count), jnp.bfloat16),
                pltpu.VMEM((row_devices, FB, row_count // FB), jnp.bfloat16),
                pltpu.VMEM((moved, row_count), jnp.bfloat16),
                pltpu.VMEM((row_devices, moved, capacity), jnp.bfloat16),
                pltpu.VMEM((row_devices, moved, capacity), jnp.bfloat16),
                pltpu.VMEM((NL * width_k + TAIL, FB * B), jnp.float32),
                dma((3, row_devices)),
                dma((3, row_devices)),
                dma((2, row_devices)),
                dma((2, row_devices)),
                dma((row_devices,)),
                dma((row_devices,)),
            ],
            compiler_params=pltpu.CompilerParams(
                collective_id=0, has_side_effects=True, vmem_limit_bytes=VMEM
            ),
        )(features, targets, pack, code, ranks)
        return (last_bins(large_best[None])[None], last_bins(small_best)[None])
    pack, ranks = made

    owned = lax.all_to_all(
        features.reshape(row_devices, own, row_count), "row", split_axis=0, concat_axis=0
    )
    owned = owned.reshape(row_devices, own, row_count)
    own_pad = -own % FB
    if own_pad:
        owned = jnp.pad(owned, ((0, 0), (0, own_pad), (0, 0)))

    gathered = lax.all_gather(pack, "row", axis=0)

    outgoing = pl.pallas_call(
        compact_kernel,
        grid=(row_devices,),
        in_specs=[
            pl.BlockSpec((pack_rows, row_count), lambda d: (0, 0)),
            pl.BlockSpec((feat_count, row_count), lambda d: (0, 0)),
            pl.BlockSpec((1, 1, row_count), lambda d: (d, 0, 0)),
        ],
        out_specs=pl.BlockSpec((1, pack_rows + feat_count, capacity), lambda d: (d, 0, 0)),
        out_shape=jax.ShapeDtypeStruct(
            (row_devices, pack_rows + feat_count, capacity), jnp.bfloat16
        ),
        compiler_params=params,
        cost_estimate=pl.CostEstimate(
            flops=2 * 256 * row_count * row_devices * capacity,
            bytes_accessed=4 * (pack_rows + feat_count) * row_count,
            transcendentals=0,
        ),
    )(pack, features, ranks)
    arrived = lax.all_to_all(outgoing, "row", split_axis=0, concat_axis=0)
    arrived = arrived.reshape(row_devices, pack_rows + feat_count, capacity)
    per_step = row_devices
    if capacity % 128:
        arrived = arrived.transpose(1, 0, 2).reshape(1, -1, row_devices * capacity)
        per_step = 1
    small_gain = node_gains(arrived, arrived, pack_rows, feat_count, 2, width_k, per_step)
    turn = [(g, (g + 1) % leaf_devices) for g in range(leaf_devices)]
    small_gain = lax.ppermute(small_gain, "leaf", turn)[None]

    large_gain = node_gains(gathered, owned, 0, own + own_pad, 1, width_k, 1)[None, :, :own]
    return (large_gain, small_gain)


def solution(mesh):
    placed = (
        P(None, ("dom", "row")),
        P(None, ("dom", "row")),
        P("leaf", ("dom", "row")),
        P("leaf", ("dom", "row")),
        P("leaf", "dom"),
        P("leaf", "dom"),
    )
    return jax.shard_map(
        local,
        mesh=mesh,
        in_specs=placed,
        out_specs=(P("leaf", "dom", "row"), P("leaf", "row", "dom")),
        check_vma=False,
    )
```

```python
import functools

import jax
import jax.numpy as jnp
from jax import lax
from jax.experimental import pallas as pl
from jax.experimental.pallas import tpu as pltpu
from jax.sharding import PartitionSpec as P

B = 64
NL = 4
SB = 4
FB = 16
TAIL = 16
NT = (((1,), (1,)), ((), ()))
VMEM = 50 * 1024 * 1024


def prep_kernel(
    row_devices, targets_ref, boot_ref, ids_ref, table_ref, pack_ref, rank_ref, code_ref=None
):
    width_k, rows = targets_ref.shape
    weight = boot_ref[...].astype(jnp.float32)
    weighted = (targets_ref[...].astype(jnp.float32) * weight).astype(jnp.bfloat16)
    nodes = table_ref.shape[1]
    node_hot = lax.broadcasted_iota(jnp.int32, (nodes, rows), 0) == ids_ref[...]
    node_hot = jnp.where(node_hot, 1.0, 0.0).astype(jnp.bfloat16)
    found = jnp.dot(table_ref[...], node_hot, preferred_element_type=jnp.float32)
    is_large = found[0:1] > 0.5
    place = found[1:2].astype(jnp.int32)
    large_label = jnp.where(is_large, place, NL).astype(jnp.float32)
    slot_label = (place % SB).astype(jnp.float32)
    dest = jnp.where(is_large, row_devices, place // SB)
    tail_row = lax.broadcasted_iota(jnp.int32, (TAIL, rows), 0)
    tail = jnp.where(tail_row == 0, weight, 0.0)
    tail = jnp.where(tail_row == 1, large_label, tail)
    tail = jnp.where(tail_row == 2, slot_label, tail)
    pack_ref[0:width_k, :] = weighted
    pack_ref[width_k : width_k + TAIL, :] = tail.astype(jnp.bfloat16)
    if code_ref is not None:
        code = weight + 4.0 * large_label
        wide = rows // FB
        code = jnp.concatenate(
            [code[:, c * wide : (c + 1) * wide] for c in range(FB)], axis=0
        )
        code_ref[...] = code.astype(jnp.bfloat16)
    dest_rows = rank_ref.shape[0]
    step = 512
    earlier = lax.broadcasted_iota(jnp.int32, (step, step), 0) < lax.broadcasted_iota(
        jnp.int32, (step, step), 1
    )
    earlier = jnp.where(earlier, 1.0, 0.0).astype(jnp.bfloat16)
    carry = jnp.zeros((dest_rows, 1), jnp.float32)
    for at in range(0, rows, step):
        hot = lax.broadcasted_iota(jnp.int32, (dest_rows, step), 0) == dest[:, at : at + step]
        hot_f = jnp.where(hot, 1.0, 0.0)
        before = jnp.dot(hot_f.astype(jnp.bfloat16), earlier, preferred_element_type=jnp.float32)
        ranks = jnp.where(hot, before + carry, -1.0)
        rank_ref[:, 0, at : at + step] = ranks
        carry = carry + jnp.sum(hot_f, axis=1, keepdims=True)


def compact_kernel(pack_ref, features_ref, rank_ref, out_ref):
    rows = features_ref.shape[1]
    capacity = out_ref.shape[2]
    spots = lax.broadcasted_iota(jnp.int32, (capacity, 128), 0).astype(jnp.float32)
    spots = spots.astype(jnp.bfloat16)[:, 0:1]
    ranks = rank_ref[0].astype(jnp.bfloat16)
    hot = jnp.where(spots == ranks, 1.0, 0.0).astype(jnp.bfloat16)
    payload = jnp.concatenate([pack_ref[...], features_ref[...]], axis=0)
    moved = lax.dot_general(payload, hot, NT, preferred_element_type=jnp.float32)
    out_ref[0] = moved.astype(jnp.bfloat16)


def chunk_sums(weighted, weight, label, values):
    step = values.shape[1]
    parts = [weighted * jnp.where(label == n, 1.0, 0.0).astype(jnp.bfloat16) for n in range(NL)]
    node_row = lax.broadcasted_iota(jnp.int32, (TAIL, step), 0).astype(jnp.float32)
    parts.append(jnp.where(node_row == label, weight, 0.0).astype(jnp.bfloat16))
    columns = jnp.concatenate(parts, axis=0)
    tall = jnp.concatenate([values] * (128 // FB), axis=0).T
    one = jnp.ones_like(tall)
    zero = jnp.zeros_like(tall)
    bins = lax.broadcasted_iota(jnp.int32, (1, 128), 1) // FB
    masks = []
    for first in range(0, B, 128 // FB):
        u = bins + first
        edge = (u - (B // 2 - 1)).astype(jnp.float32) / 16.0
        edge = jnp.where(u == B - 1, jnp.inf, edge).astype(jnp.bfloat16)
        masks.append(jnp.where(tall < edge, one, zero))
    below = jnp.concatenate(masks, axis=1)
    return jnp.dot(columns, below, preferred_element_type=jnp.float32)


def best_scores(acc_ref, width_k):
    wide = 128
    sums = NL * width_k
    pick = lax.broadcasted_iota(jnp.int32, (wide, wide), 0) == (
        wide - FB + lax.broadcasted_iota(jnp.int32, (wide, wide), 1) % FB
    )
    whole = jnp.dot(
        acc_ref[:, FB * B - wide : FB * B],
        jnp.where(pick, 1.0, 0.0),
        precision=lax.Precision.HIGHEST,
        preferred_element_type=jnp.float32,
    )
    whole_sum = whole[0:sums]
    whole_cnt = whole[sums : sums + 8]

    def term(vec, cnt):
        rows = []
        for n in range(NL):
            part = vec[n * width_k : (n + 1) * width_k]
            rows.append(jnp.sum(part * part, axis=0, keepdims=True))
        return jnp.concatenate(rows, axis=0) / jnp.maximum(cnt[0:NL], 1.0)

    whole_term = term(whole_sum, whole_cnt)
    best = None
    for start in range(0, FB * B, wide):
        left_sum = acc_ref[0:sums, start : start + wide]
        left_cnt = acc_ref[sums : sums + 8, start : start + wide]
        score = term(left_sum, left_cnt) + term(whole_sum - left_sum, whole_cnt - left_cnt)
        score = score - whole_term
        if start == FB * B - wide:
            lane = lax.broadcasted_iota(jnp.int32, (NL, wide), 1)
            score = jnp.where(lane < wide - FB, score, -jnp.inf)
        best = score if best is None else jnp.maximum(best, score)
    return best / width_k


def gain_kernel(width_k, label_row, pack_ref, features_ref, out_ref, acc_ref):
    at = pl.program_id(1)
    sources, _, rows = features_ref.shape
    step = min(rows, 512)

    @pl.when(at == 0)
    def _():
        acc_ref[...] = jnp.zeros_like(acc_ref)

    total = acc_ref[...]
    for source in range(sources):
        for start in range(0, rows, step):
            cut = pl.ds(start, step)
            tail = pack_ref[source, width_k : width_k + TAIL, cut].astype(jnp.float32)
            total = total + chunk_sums(
                pack_ref[source, 0:width_k, cut],
                tail[0:1],
                tail[label_row : label_row + 1],
                features_ref[source, :, cut],
            )
    acc_ref[...] = total

    @pl.when(at == pl.num_programs(1) - 1)
    def _():
        out_ref[0] = best_scores(acc_ref, width_k)


def flipped(index, mask, count):
    out, bit = 0, 1
    while bit < count:
        out = out + bit * lax.rem(index // bit + mask // bit, 2)
        bit *= 2
    return out


def level_kernel(
    n_row,
    feat_ref,
    targ_ref,
    pack_ref,
    code_ref,
    rank_ref,
    large_ref,
    small_ref,
    owned,
    targs,
    codes,
    payload,
    outgoing,
    arrived,
    acc_ref,
    send_sem,
    recv_sem,
    pass_send,
    pass_recv,
    small_send,
    small_recv,
):
    width_k, rows = targ_ref.shape
    feat_count = feat_ref.shape[0]
    pack_rows = width_k + TAIL
    capacity = outgoing.shape[2]
    me = lax.axis_index("row")
    leaf = lax.axis_index("leaf")
    other = 1 - leaf
    half = rows // 2
    mine = pl.ds(pl.multiple_of(leaf * half, 128), half)

    barrier = pltpu.get_barrier_semaphore()

    def greet(i, _):
        peer = lax.rem(me + i, n_row)
        pl.semaphore_signal(barrier, inc=1, device_id={"row": peer, "leaf": leaf})
        pl.semaphore_signal(barrier, inc=1, device_id={"row": peer, "leaf": other})
        return 0

    lax.fori_loop(1, n_row, greet, 0)
    pl.semaphore_signal(barrier, inc=1, device_id={"row": me, "leaf": other})
    pl.semaphore_wait(barrier, 2 * n_row - 1)

    def first(i):
        peer = flipped(me, i, n_row)
        block = pl.ds(pl.multiple_of(peer * FB, FB), FB)
        pairs = (
            (feat_ref.at[block, mine], owned.at[me, :, mine]),
            (targ_ref.at[:, mine], targs.at[me, :, mine]),
            (code_ref, codes.at[me]),
        )
        return [
            pltpu.make_async_remote_copy(
                src_ref=src,
                dst_ref=dst,
                send_sem=send_sem.at[k, i],
                recv_sem=recv_sem.at[k, i],
                device_id={"row": peer, "leaf": leaf},
            )
            for k, (src, dst) in enumerate(pairs)
        ]

    def handed(i):
        source = flipped(me, i, n_row)
        return [
            pltpu.make_async_remote_copy(
                src_ref=buf.at[source, :, mine],
                dst_ref=buf.at[source, :, mine],
                send_sem=pass_send.at[k, i],
                recv_sem=pass_recv.at[k, i],
                device_id={"row": me, "leaf": other},
            )
            for k, buf in enumerate((owned, targs))
        ]

    def passed(i, b):
        source = flipped(me, i, n_row)
        return pltpu.make_async_remote_copy(
            src_ref=targs.at[source, :, mine],
            dst_ref=targs.at[source, :, mine],
            send_sem=send_sem.at[1, i + b],
            recv_sem=recv_sem.at[1, i + b],
            device_id={"row": flipped(me, b, n_row), "leaf": leaf},
        )

    def small_copy(i):
        peer = lax.rem(me + i, n_row)
        return pltpu.make_async_remote_copy(
            src_ref=outgoing.at[peer],
            dst_ref=arrived.at[me],
            send_sem=small_send.at[i],
            recv_sem=small_recv.at[i],
            device_id={"row": peer, "leaf": other},
        )

    for i in (4, 2, 1):
        for copy in first(i):
            copy.start()
    for i in (6, 5, 3, 7):
        feature_copy, _, code_copy = first(i)
        feature_copy.start()
        code_copy.start()
    payload[0:pack_rows, :] = pack_ref[...]
    payload[pack_rows : pack_rows + feat_count, :] = feat_ref[...]
    owned[me] = feat_ref[pl.ds(pl.multiple_of(me * FB, FB), FB), :]
    targs[me] = targ_ref[...]
    codes[me] = code_ref[...]
    acc_ref[...] = jnp.zeros_like(acc_ref)

    def compact(i, _):
        peer = lax.rem(me + i, n_row)
        lane = lax.broadcasted_iota(jnp.int32, (1, 128), 1).astype(jnp.float32)
        moved = jnp.zeros((pack_rows + feat_count, capacity), jnp.float32)
        step = 512
        for at in range(0, rows, step):
            ranks = rank_ref[peer, :, at : at + step].astype(jnp.bfloat16)
            tall = jnp.broadcast_to(ranks, (128, step)).T
            hot = [
                jnp.where(tall == (lane + c).astype(jnp.bfloat16), 1.0, 0.0).astype(jnp.bfloat16)
                for c in range(0, capacity, 128)
            ]
            moved = moved + jnp.dot(
                payload[:, at : at + step],
                jnp.concatenate(hot, axis=1),
                preferred_element_type=jnp.float32,
            )
        outgoing[peer] = moved.astype(jnp.bfloat16)
        small_copy(i).start()
        return 0

    lax.fori_loop(0, n_row, compact, 0)

    def take(i):
        for copy in first(i):
            copy.wait_recv()
        for copy in handed(i):
            copy.start()

        @pl.when(i % 2 == 0)
        def _():
            passed(i, 1).start()

        @pl.when(i == 4)
        def _():
            passed(i, 2).start()

    def order(p):
        return 4 * (p % 2) + 2 * ((p // 2) % 2) + p // 4

    def large(p, _):
        i = order(p)

        @pl.when(p + 1 < n_row)
        def _():
            take(order(p + 1))

        @pl.when(i > 0)
        def _():
            for copy in handed(i):
                copy.wait_recv()

        source = flipped(me, i, n_row)
        code = codes[source].astype(jnp.float32)
        code = jnp.concatenate([code[c : c + 1] for c in range(FB)], axis=1)
        label = jnp.floor(code * 0.25)
        weight = code - 4.0 * label
        total = acc_ref[...]
        step = 512
        for start in range(0, rows, step):
            cut = pl.ds(start, step)
            scale = weight[:, start : start + step]
            weighted = (targs[source, :, cut].astype(jnp.float32) * scale).astype(jnp.bfloat16)
            total = total + chunk_sums(
                weighted, scale, label[:, start : start + step], owned[source, :, cut]
            )
        acc_ref[...] = total
        return 0

    lax.fori_loop(0, n_row, large, 0)
    large_ref[...] = best_scores(acc_ref, width_k)

    def small_arrive(i, _):
        small_copy(i).wait_recv()
        return 0

    lax.fori_loop(0, n_row, small_arrive, 0)

    def small(j, _):
        total = jnp.zeros_like(acc_ref)
        block = pl.ds(pl.multiple_of(pack_rows + j * FB, FB), FB)
        for source in range(n_row):
            tail = arrived[source, width_k:pack_rows, :].astype(jnp.float32)
            total = total + chunk_sums(
                arrived[source, 0:width_k, :], tail[0:1], tail[2:3], arrived[source, block, :]
            )
        acc_ref[...] = total
        small_ref[j] = best_scores(acc_ref, width_k)
        return 0

    lax.fori_loop(0, feat_count // FB, small, 0)

    def finish(i, _):
        for copy in first(i) + handed(i):
            copy.wait_send()
        return 0

    lax.fori_loop(1, n_row, finish, 0)

    def finish_small(i, _):
        small_copy(i).wait_send()
        return 0

    lax.fori_loop(0, n_row, finish_small, 0)


def last_bins(best):
    blocks = best.shape[0]
    best = jnp.max(best.reshape(blocks, NL, 128 // FB, FB), axis=2)
    return best.transpose(1, 0, 2).reshape(NL, blocks * FB)


def node_gains(pack, features, feat_row, feat_count, label_row, width_k, per_step):
    sources, pack_rows, rows = pack.shape[0], width_k + TAIL, pack.shape[2]
    blocks = feat_count // FB
    best = pl.pallas_call(
        functools.partial(gain_kernel, width_k, label_row),
        grid=(blocks, sources // per_step),
        in_specs=[
            pl.BlockSpec((per_step, pack_rows, rows), lambda j, i: (i, 0, 0)),
            pl.BlockSpec((per_step, FB, rows), lambda j, i: (i, feat_row // FB + j, 0)),
        ],
        out_specs=pl.BlockSpec((1, NL, 128), lambda j, i: (j, 0, 0)),
        out_shape=jax.ShapeDtypeStruct((blocks, NL, 128), jnp.float32),
        scratch_shapes=[pltpu.VMEM((NL * width_k + TAIL, FB * B), jnp.float32)],
        compiler_params=pltpu.CompilerParams(vmem_limit_bytes=VMEM),
        cost_estimate=pl.CostEstimate(
            flops=2 * feat_count * B * 144 * sources * rows,
            bytes_accessed=2 * sources * rows * (feat_count + 48),
            transcendentals=0,
        ),
    )(pack, features)
    return last_bins(best)


def local(features, targets, bootstrap, node_ids, node_flags, node_place):
    feat_count, row_count = features.shape
    width_k = targets.shape[0]
    row_devices = lax.axis_size("row")
    leaf_devices = lax.axis_size("leaf")
    capacity = row_count // (2 * row_devices)
    own = feat_count // row_devices
    pack_rows = width_k + TAIL

    nodes = node_flags.shape[1]
    table = jnp.concatenate([node_flags, node_place], axis=0).astype(jnp.bfloat16)
    table = jnp.pad(table, ((0, 14), (0, -nodes % 16)))
    params = pltpu.CompilerParams(vmem_limit_bytes=VMEM)
    fused = own == FB and capacity % 128 == 0 and leaf_devices == 2
    fused = fused and row_devices == 8
    shapes = [
        jax.ShapeDtypeStruct((pack_rows, row_count), jnp.bfloat16),
        jax.ShapeDtypeStruct((row_devices, 1, row_count), jnp.float32),
    ]
    if fused:
        shapes.append(jax.ShapeDtypeStruct((FB, row_count // FB), jnp.bfloat16))
    made = pl.pallas_call(
        functools.partial(prep_kernel, row_devices), out_shape=shapes, compiler_params=params
    )(targets, bootstrap, node_ids, table)
    if fused:
        pack, ranks, code = made
        moved = pack_rows + feat_count
        dma = pltpu.SemaphoreType.DMA
        large_best, small_best = pl.pallas_call(
            functools.partial(level_kernel, row_devices),
            out_shape=(
                jax.ShapeDtypeStruct((NL, 128), jnp.float32),
                jax.ShapeDtypeStruct((feat_count // FB, NL, 128), jnp.float32),
            ),
            in_specs=[pl.BlockSpec(memory_space=pltpu.VMEM)] * 5,
            out_specs=(pl.BlockSpec(memory_space=pltpu.VMEM),) * 2,
            scratch_shapes=[
                pltpu.VMEM((row_devices, FB, row_count), jnp.bfloat16),
                pltpu.VMEM((row_devices, width_k, row_count), jnp.bfloat16),
                pltpu.VMEM((row_devices, FB, row_count // FB), jnp.bfloat16),
                pltpu.VMEM((moved, row_count), jnp.bfloat16),
                pltpu.VMEM((row_devices, moved, capacity), jnp.bfloat16),
                pltpu.VMEM((row_devices, moved, capacity), jnp.bfloat16),
                pltpu.VMEM((NL * width_k + TAIL, FB * B), jnp.float32),
                dma((3, row_devices)),
                dma((3, row_devices)),
                dma((2, row_devices)),
                dma((2, row_devices)),
                dma((row_devices,)),
                dma((row_devices,)),
            ],
            compiler_params=pltpu.CompilerParams(
                collective_id=0, has_side_effects=True, vmem_limit_bytes=VMEM
            ),
        )(features, targets, pack, code, ranks)
        return (last_bins(large_best[None])[None], last_bins(small_best)[None])
    pack, ranks = made

    owned = lax.all_to_all(
        features.reshape(row_devices, own, row_count), "row", split_axis=0, concat_axis=0
    )
    owned = owned.reshape(row_devices, own, row_count)
    own_pad = -own % FB
    if own_pad:
        owned = jnp.pad(owned, ((0, 0), (0, own_pad), (0, 0)))

    gathered = lax.all_gather(pack, "row", axis=0)

    outgoing = pl.pallas_call(
        compact_kernel,
        grid=(row_devices,),
        in_specs=[
            pl.BlockSpec((pack_rows, row_count), lambda d: (0, 0)),
            pl.BlockSpec((feat_count, row_count), lambda d: (0, 0)),
            pl.BlockSpec((1, 1, row_count), lambda d: (d, 0, 0)),
        ],
        out_specs=pl.BlockSpec((1, pack_rows + feat_count, capacity), lambda d: (d, 0, 0)),
        out_shape=jax.ShapeDtypeStruct(
            (row_devices, pack_rows + feat_count, capacity), jnp.bfloat16
        ),
        compiler_params=params,
        cost_estimate=pl.CostEstimate(
            flops=2 * 256 * row_count * row_devices * capacity,
            bytes_accessed=4 * (pack_rows + feat_count) * row_count,
            transcendentals=0,
        ),
    )(pack, features, ranks)
    arrived = lax.all_to_all(outgoing, "row", split_axis=0, concat_axis=0)
    arrived = arrived.reshape(row_devices, pack_rows + feat_count, capacity)
    per_step = row_devices
    if capacity % 128:
        arrived = arrived.transpose(1, 0, 2).reshape(1, -1, row_devices * capacity)
        per_step = 1
    small_gain = node_gains(arrived, arrived, pack_rows, feat_count, 2, width_k, per_step)
    turn = [(g, (g + 1) % leaf_devices) for g in range(leaf_devices)]
    small_gain = lax.ppermute(small_gain, "leaf", turn)[None]

    large_gain = node_gains(gathered, owned, 0, own + own_pad, 1, width_k, 1)[None, :, :own]
    return (large_gain, small_gain)


def solution(mesh):
    placed = (
        P(None, ("dom", "row")),
        P(None, ("dom", "row")),
        P("leaf", ("dom", "row")),
        P("leaf", ("dom", "row")),
        P("leaf", "dom"),
        P("leaf", "dom"),
    )
    return jax.shard_map(
        local,
        mesh=mesh,
        in_specs=placed,
        out_specs=(P("leaf", "dom", "row"), P("leaf", "row", "dom")),
        check_vma=False,
    )
```
